32 devices in a mesh: expert: 8 (over y, x, core), tensor: 4 (over z).
Axes of the slice: x: 2, y: 2, z: 4, core: 2. Of those that a mesh axis runs over, the one named last changes fastest.
Arguments:
- tokens: bfloat16 [4096, 2048], P('expert'), may hold values from -6 to 6
- sequence_numbers: int32 [4096], P('expert'), may hold values from 0 to 7, as said below
- routes: int32 [4096, 8], P('expert'), may hold values from 0 to 15, all different within a row; in each aligned block of 512 rows (0 to 511, 512 to 1023, ...) at most 384 rows name the same one
- attn_gain: float32 [2048], replicated, may hold values from 0.5 to 1.5
- w_query: bfloat16 [2048, 4096], P(None, 'tensor'), may hold values from -0.125 to 0.125
- key_projection: bfloat16 [2048, 512], P(None, 'tensor'), may hold values from -0.125 to 0.125
- value_projection: bfloat16 [2048, 512], P(None, 'tensor'), may hold values from -0.125 to 0.125
- query_gain: float32 [128], replicated, may hold values from 0.5 to 1.5
- key_gain: float32 [128], replicated, may hold values from 0.5 to 1.5
- w_out: bfloat16 [4096, 2048], P('tensor'), may hold values from -0.5 to 0.5
- moe_gain: float32 [2048], replicated, may hold values from 0.5 to 1.5
- w_router: bfloat16 [2048, 16], replicated, may hold values from -0.0625 to 0.0625
- w_gate: bfloat16 [16, 2048, 768], P('expert', None, 'tensor'), may hold values from -0.125 to 0.125
- w_up: bfloat16 [16, 2048, 768], P('expert', None, 'tensor'), may hold values from -0.125 to 0.125
- w_down: bfloat16 [16, 768, 2048], P('expert', 'tensor'), may hold values from -0.875 to 0.875
- cotangent: bfloat16 [4096, 2048], P('expert', 'tensor'), may hold values from -6 to 6
Outputs:
- block_out: bfloat16 [4096, 2048], P('expert', 'tensor')
- input_grad: float32 [4096, 2048], P('expert', 'tensor')
- attn_gain_grad: float32 [2048], P('expert')
- query_weight_grad: float32 [2048, 4096], P('expert', 'tensor')
- key_weight_grad: float32 [2048, 512], P('expert', 'tensor')
- value_weight_grad: float32 [2048, 512], P('expert', 'tensor')
- query_gain_grad: float32 [128], P('expert')
- key_gain_grad: float32 [128], P('expert')
- out_weight_grad: float32 [4096, 2048], P('tensor', 'expert')
- moe_gain_grad: float32 [2048], P('expert')
- router_grad: float32 [2048, 16], P('expert')
- gate_grad: float32 [16, 2048, 768], P('expert', None, 'tensor')
- up_grad: float32 [16, 2048, 768], P('expert', None, 'tensor')
- down_grad: float32 [16, 768, 2048], P('expert', 'tensor')
The draws below stay inside these ranges and needn't reach their ends.
Inputs may be any that keep to these rules, and one draw needn't show every extreme that they name: `sequence_numbers`: inside each device's 512 rows the numbers start at 0 and rise by one where a new sequence begins; a device holds 1 to 8 sequences, some device a single one of 512 tokens and some device 8. `routes`: among the rows of one device no expert is named by more than 384 rows, a bound that some block reaches.
All inputs are finite; a program needn't handle non-finite values.
Results may differ from the reference program's by a relative error of at most 0.024.
Values may be sent and summed in bfloat16 or wider, within the bound.
No kernel may reach another device: no remote copies, remote signals or barrier semaphores. Data moves between devices by JAX's collectives and lax.ppermute only.
A program may use at most 384 MiB of HBM per device.

```python
import math
import jax
import jax.numpy as jnp
import numpy as np
from jax import lax

MODEL_DIM = 2048
QUERY_HEADS = 32
KEY_VALUE_HEADS = 4
HEAD_SIZE = 128
FFE = 768
TOP = 8
TOKENS_PER_SHARD = 512
TOKEN_TOTAL = 4096
EXPERTS = 16
CAP = 384
N_TENSOR = 4


def draw_sequence_numbers(key, part):
    devices = TOKEN_TOTAL // TOKENS_PER_SHARD
    key_count, key_first, key_perm = jax.random.split(key, 3)
    cut_counts = jax.random.randint(key_count, (devices,), 0, 8)
    first_device = jax.random.randint(key_first, (), 0, devices)
    device_ids = jnp.arange(devices)
    cut_counts = jnp.where(device_ids == first_device, 0, cut_counts)
    cut_counts = jnp.where(device_ids == (first_device + 1) % devices, 7, cut_counts)
    device_keys = jax.random.split(key_perm, devices)

    def one_device(device_key, cuts):
        shuffled = jax.random.permutation(device_key, TOKENS_PER_SHARD - 1) + 1
        taken = (jnp.arange(TOKENS_PER_SHARD - 1) < cuts).astype(jnp.int32)
        marks = jnp.zeros((TOKENS_PER_SHARD,), jnp.int32).at[shuffled].add(taken)
        return jnp.cumsum(marks).astype(jnp.int32)
    return jax.vmap(one_device)(device_keys, cut_counts).reshape(TOKEN_TOTAL).astype(jnp.int32)


def steps_of(rng, extent, cuts, low, high):
    def one(axis_at, shards_of):
        steps = jax.random.uniform(jax.random.fold_in(jax.random.fold_in(rng, 6), axis_at), (shards_of,), jnp.float32, low / len(cuts), high / len(cuts))
        return jnp.repeat(jnp.exp(steps), extent[axis_at] // shards_of).reshape((-1,) + (1,) * (len(extent) - axis_at - 1))

    level = one(*cuts[0])
    for cut in cuts[1:]:
        level = level * one(*cut)
    return level


def shared_out(own_key, own, number, rows, number_of, top, most, slope):
    sequence = jax.random.permutation(own_key, number_of)
    crowded, ordinary = portions_of(number_of, rows * top, most, slope, True), portions_of(number_of, rows * top, most, slope, False)
    places = jnp.arange(number_of)

    def named(tallies, turn):
        used = int((tallies > 0).sum())
        fixed = max(1, used // 4)
        moved = fixed + (places - fixed + turn * (used - fixed)) % max(1, number_of - fixed)
        return jnp.zeros((number_of,), jnp.int32).at[sequence[jnp.where(places < fixed, places, moved)]].set(jnp.asarray(tallies, jnp.int32))

    tallies = jnp.where(number % 4 == 0, named(crowded, number // 4), named(ordinary, number - number // 4 - 1))
    mixed = jax.random.permutation(jax.random.fold_in(own, 3), number_of)
    source_of, sink = mixed[0:number_of // 2 * 2:2], mixed[1:number_of // 2 * 2:2]
    margin = jnp.minimum(tallies[source_of] - 1, most - tallies[sink]) // 2
    margin = jnp.where((source_of == sequence[0]) | (sink == sequence[0]) | (tallies[sink] == 0), 0, jnp.maximum(margin, 0))
    moved = jax.random.randint(jax.random.fold_in(own, 4), (number_of // 2,), 0, 1 << 20) % (margin + 1)
    tallies = tallies.at[source_of].add(-moved).at[sink].add(moved)
    labels = jnp.searchsorted(jnp.cumsum(tallies), jnp.arange(rows * top), side="right").astype(jnp.int32)
    listing = labels.reshape(top, rows).T
    listing = listing[jax.random.permutation(jax.random.fold_in(own, 1), rows)]
    turn = jax.random.randint(jax.random.fold_in(own, 2), (rows, 1), 0, top)
    return jnp.take_along_axis(listing, (jnp.arange(top)[None, :] + turn) % top, axis=1)


def portions_of(number_of, total, bound, lean, full):
    loads = [(1 << 20) // math.isqrt(rank ** lean) + 1 for rank in range(1, number_of + 1)]
    largest = bound if full else min(bound, max(-(-total // number_of), total * loads[0] // sum(loads)))
    least = 1 if total - largest >= number_of - 1 else 0
    counts, rest = [largest] + [least] * (number_of - 1), total - largest - least * (number_of - 1)
    while rest > 0:
        free = [i for i in range(1, number_of) if counts[i] < largest] or [i for i in range(1, number_of) if counts[i] < bound]
        pool, budget = sum([loads[i] for i in free]), rest
        for i in free:
            extra = min(bound - counts[i], max(1, budget * loads[i] // pool), rest)
            counts[i] = counts[i] + extra
            rest = rest - extra
    return np.array(counts)


def bell_draw(key, dims, scale, reach, cuts=(), kind=jnp.bfloat16):
    loudness = steps_of(key, dims, cuts, -0.22, 0.18) if cuts else 1.0
    values = jax.random.normal(key, dims, jnp.float32) * scale * loudness
    return jnp.minimum(jnp.maximum(values, -reach), reach).astype(kind)


def setup_inputs(seed: int = 0) -> dict:
    seeds = jax.random.split(jax.random.key(seed), 17)
    tokens = bell_draw(seeds[0], (TOKEN_TOTAL, MODEL_DIM), 1.0, 6.0, ((0, 8),))
    sequence_numbers = draw_sequence_numbers(jax.random.fold_in(seeds[16], 71), 0)
    routes_keys = jax.random.split(jax.random.fold_in(seeds[2], 1), TOKEN_TOTAL // TOKENS_PER_SHARD)
    routes_turns = jax.random.permutation(jax.random.fold_in(seeds[2], 3), TOKEN_TOTAL // TOKENS_PER_SHARD)
    routes = jax.vmap(lambda own, number: shared_out(jax.random.fold_in(seeds[2], 2), own, number, TOKENS_PER_SHARD, EXPERTS, TOP, CAP, 2))(routes_keys, routes_turns).reshape((TOKEN_TOTAL, TOP))
    attn_gain = jnp.clip(1.0 + 0.1 * jax.random.normal(seeds[3], (MODEL_DIM,), jnp.float32), 0.5, 1.5)
    w_query = bell_draw(seeds[4], (MODEL_DIM, QUERY_HEADS * HEAD_SIZE), MODEL_DIM ** -0.5, 0.125, ((1, 4),))
    key_projection = bell_draw(seeds[5], (MODEL_DIM, KEY_VALUE_HEADS * HEAD_SIZE), MODEL_DIM ** -0.5, 0.125, ((1, 4),))
    value_projection = bell_draw(seeds[6], (MODEL_DIM, KEY_VALUE_HEADS * HEAD_SIZE), MODEL_DIM ** -0.5, 0.125, ((1, 4),))
    query_gain = jnp.clip(1.0 + 0.1 * jax.random.normal(seeds[7], (HEAD_SIZE,), jnp.float32), 0.5, 1.5)
    key_gain = jnp.clip(1.0 + 0.1 * jax.random.normal(seeds[8], (HEAD_SIZE,), jnp.float32), 0.5, 1.5)
    w_out = bell_draw(seeds[9], (QUERY_HEADS * HEAD_SIZE, MODEL_DIM), (QUERY_HEADS * HEAD_SIZE // 32) ** -0.5, 0.5, ((0, 4),))
    moe_gain = jnp.clip(1.0 + 0.1 * jax.random.normal(seeds[10], (MODEL_DIM,), jnp.float32), 0.5, 1.5)
    w_router = bell_draw(seeds[11], (MODEL_DIM, EXPERTS), (4 * MODEL_DIM) ** -0.5, 0.0625)
    w_gate = bell_draw(seeds[12], (EXPERTS, MODEL_DIM, FFE), MODEL_DIM ** -0.5, 0.125, ((0, 8), (2, 4)))
    w_up = bell_draw(seeds[13], (EXPERTS, MODEL_DIM, FFE), MODEL_DIM ** -0.5, 0.125, ((0, 8), (2, 4)))
    w_down = bell_draw(seeds[14], (EXPERTS, FFE, MODEL_DIM), (FFE // 16) ** -0.5, 0.875, ((0, 8), (1, 4)))
    cotangent = bell_draw(seeds[15], (TOKEN_TOTAL, MODEL_DIM), 1.0, 6.0, ((0, 8), (1, 4)))
    return {"tokens": tokens, "sequence_numbers": sequence_numbers, "routes": routes, "attn_gain": attn_gain, "w_query": w_query, "key_projection": key_projection, "value_projection": value_projection, "query_gain": query_gain, "key_gain": key_gain, "w_out": w_out, "moe_gain": moe_gain, "w_router": w_router, "w_gate": w_gate, "w_up": w_up, "w_down": w_down, "cotangent": cotangent}


@jax.custom_vjp
def reduced_copy(v):
    return lax.optimization_barrier(v.astype(jnp.bfloat16)).astype(jnp.float32)

@jax.custom_vjp
def reduced_backward(v):
    return v

def low_keep(v):
    return (reduced_copy(v), None)

def low_pass(kept, grad):
    return (grad,)

def back_keep(v):
    return (v, None)

def back_low(kept, grad):
    return (reduced_copy(grad),)
reduced_copy.defvjp(low_keep, low_pass)
reduced_backward.defvjp(back_keep, back_low)

def matrix_product(left, right):
    return jnp.dot(left, right, precision=lax.Precision.HIGHEST)

def rms_norm(values, gain_vec):
    return values * lax.rsqrt(lax.optimization_barrier(jnp.mean(values * values, axis=-1, keepdims=True)) + 1e-06) * gain_vec

def rotate(values, cos_table, sine_table):
    half_dim = values.shape[-1] // 2
    first_half = values[..., :half_dim]
    second = values[..., half_dim:]
    return jnp.concatenate([first_half * cos_table - second * sine_table, second * cos_table + first_half * sine_table], axis=-1)

def rope_tables(positions, head_dim):
    half_dim = head_dim // 2
    frequency = jnp.power(1000000.0, -2.0 * jnp.arange(half_dim).astype(jnp.float32) / head_dim)
    angles = positions.astype(jnp.float32)[:, None] * frequency[None, :]
    return (jnp.cos(angles)[:, None, :], jnp.sin(angles)[:, None, :])

def seq_positions(sequence_numbers, block_len):
    total_len = sequence_numbers.shape[0]
    places = jnp.arange(total_len).astype(jnp.int32)
    previous = jnp.concatenate([sequence_numbers[:1] - 1, sequence_numbers[:-1]])
    starts = (places % block_len == 0) | (sequence_numbers != previous)
    first_place = lax.cummax(jnp.where(starts, places, 0), axis=0)
    return places - first_place

def attend_block(query_block, key_block, value_block, seg_block):
    tok_len = query_block.shape[0]
    kv_heads = key_block.shape[1]
    head_dim = query_block.shape[-1]
    group_size = query_block.shape[1] // kv_heads
    grouped = query_block.reshape(tok_len, kv_heads, group_size, head_dim)
    scores = jnp.einsum('qhgd,khd->hgqk', grouped, key_block, precision=lax.Precision.HIGHEST) * head_dim ** (-0.5)
    scores = reduced_backward(scores)
    places = jnp.arange(tok_len).astype(jnp.int32)
    allowed = (seg_block[:, None] == seg_block[None, :]) & (places[:, None] >= places[None, :])
    scores = jnp.where(allowed, scores, -1e+30)
    probabilities = reduced_copy(jax.nn.softmax(scores, axis=-1))
    attention_output = jnp.einsum('hgqk,khd->qhgd', probabilities, value_block, precision=lax.Precision.HIGHEST)
    return attention_output.reshape(tok_len, kv_heads * group_size * head_dim)

def attention_parts(pieces):
    return attend_block(pieces[0], pieces[1], pieces[2], pieces[3])

def reference(tokens, sequence_numbers, routes, attn_gain, w_query, key_projection, value_projection, query_gain, key_gain, w_out, moe_gain, w_router, w_gate, w_up, w_down, cotangent):
    positions = seq_positions(sequence_numbers, TOKENS_PER_SHARD)
    cos_table, sine_table = rope_tables(positions, HEAD_SIZE)
    block_list = TOKEN_TOTAL // TOKENS_PER_SHARD
    fwidth = FFE // N_TENSOR
    expert_ids = jnp.arange(EXPERTS).astype(jnp.int32)

    def forward(inputs, attn_gain, w_query, key_projection, value_projection, query_gain, key_gain, w_out, moe_gain, w_router, w_gate, w_up, w_down):
        first_hidden = reduced_copy(rms_norm(inputs, attn_gain))
        query_rows = reduced_backward(matrix_product(first_hidden, w_query)).reshape(TOKEN_TOTAL, QUERY_HEADS, HEAD_SIZE)
        key_matrix = reduced_backward(matrix_product(first_hidden, key_projection)).reshape(TOKEN_TOTAL, KEY_VALUE_HEADS, HEAD_SIZE)
        value_matrix = reduced_copy(reduced_backward(matrix_product(first_hidden, value_projection))).reshape(TOKEN_TOTAL, KEY_VALUE_HEADS, HEAD_SIZE)
        query_rows = reduced_copy(rotate(rms_norm(query_rows, query_gain), cos_table, sine_table))
        key_matrix = reduced_copy(rotate(rms_norm(key_matrix, key_gain), cos_table, sine_table))
        attention_output = lax.map(jax.checkpoint(attention_parts), (query_rows.reshape(block_list, TOKENS_PER_SHARD, QUERY_HEADS, HEAD_SIZE), key_matrix.reshape(block_list, TOKENS_PER_SHARD, KEY_VALUE_HEADS, HEAD_SIZE), value_matrix.reshape(block_list, TOKENS_PER_SHARD, KEY_VALUE_HEADS, HEAD_SIZE), sequence_numbers.reshape(block_list, TOKENS_PER_SHARD)))
        attention_output = reduced_copy(reduced_backward(attention_output.reshape(TOKEN_TOTAL, QUERY_HEADS * HEAD_SIZE)))
        branch = reduced_backward(matrix_product(attention_output, w_out))
        middle = inputs + branch
        hidden_two = reduced_copy(rms_norm(middle, moe_gain))
        logits = reduced_backward(matrix_product(hidden_two, w_router))
        probabilities = jax.nn.softmax(logits, axis=-1)
        picked = (routes[:, :, None] == expert_ids[None, None, :]).astype(probabilities.dtype)
        chosen = lax.optimization_barrier(jnp.sum(picked * probabilities[:, None, :], axis=-1))
        weights = chosen / lax.optimization_barrier(jnp.sum(chosen, axis=-1, keepdims=True))
        combine = lax.optimization_barrier(jnp.sum(picked * weights[:, :, None], axis=1))

        def expert_step(running, pieces):
            gate_e, up_e, down_e, route_share = pieces
            summed = jnp.zeros_like(middle)
            for slice_index in range(N_TENSOR):
                lower = slice_index * fwidth
                copied = reduced_backward(hidden_two)
                gate_val = reduced_backward(matrix_product(copied, gate_e[:, lower:lower + fwidth]))
                up_val = reduced_backward(matrix_product(copied, up_e[:, lower:lower + fwidth]))
                activated = reduced_copy(jax.nn.silu(gate_val) * up_val)
                summed = summed + reduced_backward(reduced_copy(matrix_product(activated, down_e[lower:lower + fwidth, :])))
            return (running + route_share[:, None] * summed, None)
        mixed_out, _ = lax.scan(jax.checkpoint(expert_step), jnp.zeros_like(middle), (w_gate, w_up, w_down, combine.T))
        return middle + mixed_out
    floats = (tokens.astype(jnp.float32), attn_gain.astype(jnp.float32), w_query.astype(jnp.float32), key_projection.astype(jnp.float32), value_projection.astype(jnp.float32), query_gain.astype(jnp.float32), key_gain.astype(jnp.float32), w_out.astype(jnp.float32), moe_gain.astype(jnp.float32), w_router.astype(jnp.float32), w_gate.astype(jnp.float32), w_up.astype(jnp.float32), w_down.astype(jnp.float32))
    output, pullback = jax.vjp(forward, *floats)
    gradients = pullback(cotangent.astype(jnp.float32))
    return (output.astype(jnp.bfloat16), gradients[0], gradients[1], gradients[2], gradients[3], gradients[4], gradients[5], gradients[6], gradients[7], gradients[8], gradients[9], gradients[10], gradients[11], gradients[12])
```

```python
import functools

import jax
import jax.numpy as jnp
from jax import lax
from jax.experimental import pallas as pl
from jax.experimental.pallas import tpu as pltpu
from jax.sharding import PartitionSpec as P


def rms_norm(values, gain_vec):
    return values * lax.rsqrt(jnp.mean(values * values, axis=-1, keepdims=True) + 1e-06) * gain_vec


def rotate(values, cos_table, sine_table):
    half_dim = values.shape[-1] // 2
    first_half = values[..., :half_dim]
    second = values[..., half_dim:]
    return jnp.concatenate(
        [
            first_half * cos_table - second * sine_table,
            second * cos_table + first_half * sine_table,
        ],
        axis=-1,
    )


def rope_tables(positions, head_dim):
    half_dim = head_dim // 2
    frequency = jnp.power(1000000.0, -2.0 * jnp.arange(half_dim).astype(jnp.float32) / head_dim)
    angles = positions.astype(jnp.float32)[:, None] * frequency[None, :]
    return (jnp.cos(angles)[:, None, :], jnp.sin(angles)[:, None, :])


def seq_positions(sequence_numbers, block_len):
    total_len = sequence_numbers.shape[0]
    places = jnp.arange(total_len)
    previous = jnp.concatenate([sequence_numbers[:1] - 1, sequence_numbers[:-1]])
    starts = (places % block_len == 0) | (sequence_numbers != previous)
    first_place = lax.cummax(jnp.where(starts, places, 0), axis=0)
    return places - first_place


F32 = jnp.float32
B16 = jnp.bfloat16


def swap(values, axis, mask):
    count = lax.axis_size(axis)
    return lax.ppermute(values, axis, [(i, i ^ mask) for i in range(count)])


def bits_of(axis):
    return lax.axis_size(axis).bit_length() - 1


def gather_blocks(block, axis, dim):
    count = lax.axis_size(axis)
    me = lax.axis_index(axis)
    held = [(0, block)]
    for bit in reversed(range(bits_of(axis))):
        mask = 1 << bit
        held = held + [(d ^ mask, swap(v, axis, mask)) for d, v in held]
    size = block.shape[dim]
    shape = list(block.shape)
    shape[dim] = size * count
    whole = jnp.zeros(shape, block.dtype)
    for d, v in held:
        whole = lax.dynamic_update_slice_in_dim(whole, v, (me ^ d) * size, dim)
    return whole


def scatter_sum(pick, axis):
    count = lax.axis_size(axis)
    me = lax.axis_index(axis)
    held = {d: pick(me ^ d) for d in range(count)}
    for bit in range(bits_of(axis)):
        mask = 1 << bit
        keep = {d: v for d, v in held.items() if not d & mask}
        for d in keep:
            came = swap(held[d ^ mask].astype(B16), axis, mask)
            keep[d] = keep[d] + came.astype(F32)
        held = keep
    return held[0]


def swap_columns(rows, axis):
    count = lax.axis_size(axis)
    me = lax.axis_index(axis)
    height, width = rows.shape[0], rows.shape[1] // count
    whole = jnp.zeros((height * count, width), rows.dtype)
    for d in range(count):
        piece = lax.dynamic_slice_in_dim(rows, (me ^ d) * width, width, 1)
        if d:
            piece = swap(piece, axis, d)
        whole = lax.dynamic_update_slice_in_dim(whole, piece, (me ^ d) * height, 0)
    return whole


def sum_everywhere(values, axis):
    for bit in range(bits_of(axis)):
        values = values + swap(values, axis, 1 << bit)
    return values


def nt_dot(left, right):
    return lax.dot_general(left, right, (((1,), (1,)), ((), ())), preferred_element_type=F32)


def tn_dot(left, right):
    return lax.dot_general(left, right, (((0,), (0,)), ((), ())), preferred_element_type=F32)


def expert_kernel(
    row_tile, hidden, experts,
    ids_ref, packed_ref, dy_ref, gate_up_ref, down_ref,
    back_ref, dgu_ref, act_ref, total, route_total,
):
    step = pl.program_id(0)
    rows, width = dy_ref.shape
    pair = 2 * hidden
    extra = packed_ref.shape[1] - width

    @pl.when(step == 0)
    def _():
        total[...] = jnp.zeros_like(total)
        route_total[...] = jnp.zeros_like(route_total)

    gate_up = gate_up_ref[0]
    down = down_ref[0]
    id_a = ids_ref[2 * step]
    id_b = ids_ref[2 * step + 1]
    for tile in range(rows // row_tile):
        at = pl.ds(tile * row_tile, row_tile)
        both = nt_dot(packed_ref[at, :width], gate_up)
        gate, up = both[:, :pair], both[:, pair:]
        shares = packed_ref[at, width:].astype(F32)
        lane = lax.broadcasted_iota(jnp.int32, (row_tile, extra), 1)

        def share_of(expert):
            mine = (lane == expert) | (lane == expert + experts)
            return jnp.sum(jnp.where(mine, shares, 0.0), axis=1, keepdims=True)

        hidden_lane = lax.broadcasted_iota(jnp.int32, (row_tile, pair), 1)
        first = hidden_lane < hidden
        share = jnp.where(first, share_of(id_a), share_of(id_b))
        sig = 1.0 / (1.0 + jnp.exp(-gate))
        silu = gate * sig
        act = (silu * up).astype(B16).astype(F32)
        raw = nt_dot(dy_ref[at, :], down)
        product = act * raw
        part_a = jnp.sum(jnp.where(first, product, 0.0), axis=1, keepdims=True)
        part_b = jnp.sum(jnp.where(first, 0.0, product), axis=1, keepdims=True)
        route_total[at, :] += jnp.where(lane == id_a, part_a, 0.0) + jnp.where(
            lane == id_b, part_b, 0.0
        )
        dact = share * raw
        dgate = dact * up * (sig * (1.0 + gate * (1.0 - sig)))
        dup = dact * silu
        dgu = jnp.concatenate([dgate.astype(B16), dup.astype(B16)], axis=1)
        dgu_ref[0, at, :] = dgu
        act_ref[0, at, :] = (share * act).astype(B16)
        total[at, :] += jnp.dot(dgu, gate_up, preferred_element_type=F32)

    @pl.when(step == pl.num_programs(0) - 1)
    def _():
        back_ref[:, :width] = total[...].astype(B16)
        back_ref[:, width:] = route_total[...].astype(B16)


def expert_pass(ids, packed, dy, gate_up, down, experts):
    rows, full = packed.shape
    width = dy.shape[1]
    groups, pair2, _ = gate_up.shape
    pair = pair2 // 2
    return pl.pallas_call(
        functools.partial(expert_kernel, min(rows, 256), pair // 2, experts),
        grid_spec=pltpu.PrefetchScalarGridSpec(
            num_scalar_prefetch=1,
            grid=(groups,),
            in_specs=[
                pl.BlockSpec((rows, full), lambda d, ids: (0, 0)),
                pl.BlockSpec((rows, width), lambda d, ids: (0, 0)),
                pl.BlockSpec((1, pair2, width), lambda d, ids: (d, 0, 0)),
                pl.BlockSpec((1, pair, width), lambda d, ids: (d, 0, 0)),
            ],
            out_specs=[
                pl.BlockSpec((rows, full), lambda d, ids: (0, 0)),
                pl.BlockSpec((1, rows, pair2), lambda d, ids: (d, 0, 0)),
                pl.BlockSpec((1, rows, pair), lambda d, ids: (d, 0, 0)),
            ],
            scratch_shapes=[
                pltpu.VMEM((rows, width), F32),
                pltpu.VMEM((rows, full - width), F32),
            ],
        ),
        out_shape=[
            jax.ShapeDtypeStruct((rows, full), B16),
            jax.ShapeDtypeStruct((groups, rows, pair2), B16),
            jax.ShapeDtypeStruct((groups, rows, pair), B16),
        ],
        compiler_params=pltpu.CompilerParams(vmem_limit_bytes=56 << 20),
        cost_estimate=pl.CostEstimate(
            flops=2 * rows * width * groups * (2 * pair2 + pair),
            bytes_accessed=2 * (groups * (pair2 + pair) * (width + rows) + 4 * rows * width),
            transcendentals=rows * groups * pair,
        ),
    )(ids, packed, dy, gate_up, down)


def per_device(
    tokens,
    sequence_numbers,
    routes,
    attn_gain,
    w_query,
    key_projection,
    value_projection,
    query_gain,
    key_gain,
    w_out,
    moe_gain,
    w_router,
    w_gate,
    w_up,
    w_down,
    cotangent,
):
    tok_count, model_width = tokens.shape
    head_dim = query_gain.shape[0]
    q_heads = w_query.shape[1] // head_dim
    kv_heads = key_projection.shape[1] // head_dim
    group_size = q_heads // kv_heads
    tensor_size = lax.axis_size("tensor")
    tensor_pos = lax.axis_index("tensor")
    expert_size = lax.axis_size("expert")
    expert_pos = lax.axis_index("expert")
    local_experts = w_gate.shape[0]
    experts = local_experts * expert_size
    hidden = w_gate.shape[2]
    pair = local_experts * hidden
    score_scale = head_dim ** (-0.5)
    own_rows = tok_count // tensor_size
    row_start = tensor_pos * own_rows
    group = 2 << ((expert_size // 2).bit_length() // 2)
    rounds = expert_size // group

    def own(values):
        return lax.dynamic_slice_in_dim(values, row_start, own_rows, 0)

    gate_up_own = jnp.concatenate(
        [
            jnp.swapaxes(w_gate, 1, 2).reshape(pair, model_width),
            jnp.swapaxes(w_up, 1, 2).reshape(pair, model_width),
        ],
        axis=0,
    )
    weights_held = [(gate_up_own, w_down.reshape(pair, model_width))]
    mask = group // 2
    while mask:
        pass_on = [(swap(a, "expert", mask), swap(b, "expert", mask)) for a, b in weights_held]
        weights_held = [v for both in zip(weights_held, pass_on) for v in both]
        mask //= 2
    gate_up = jnp.stack([a for a, _ in weights_held])
    down = jnp.stack([b for _, b in weights_held])
    ids = jnp.concatenate(
        [(expert_pos ^ d) * local_experts + jnp.arange(local_experts) for d in range(group)]
    ).astype(jnp.int32)
    dy_own = gather_blocks(cotangent, "tensor", 1)
    dy_of = [dy_own] + [swap(dy_own, "expert", group * r) for r in range(1, rounds)]

    positions = seq_positions(sequence_numbers, tok_count)
    cos_table, sine_table = rope_tables(positions, head_dim)
    local_index = jnp.arange(tok_count)
    inputs = tokens.astype(F32)
    first_hidden = rms_norm(inputs, attn_gain).astype(B16)
    query_rows = jnp.dot(first_hidden, w_query, preferred_element_type=F32).reshape(
        tok_count, q_heads, head_dim
    )
    key_matrix = jnp.dot(first_hidden, key_projection, preferred_element_type=F32).reshape(
        tok_count, kv_heads, head_dim
    )
    value_matrix = (
        jnp.dot(first_hidden, value_projection, preferred_element_type=F32)
        .astype(B16)
        .reshape(tok_count, kv_heads, head_dim)
    )

    def prepare(values, gain_vec):
        return rotate(rms_norm(values, gain_vec), cos_table, sine_table)

    query_rot, pull_query = jax.vjp(prepare, query_rows, query_gain)
    key_rot, pull_key = jax.vjp(prepare, key_matrix, key_gain)
    query_low = query_rot.astype(B16).reshape(tok_count, kv_heads, group_size, head_dim)
    key_low = key_rot.astype(B16)

    def block_scores():
        scores = (
            jnp.einsum("qhgd,khd->hgqk", query_low, key_low, preferred_element_type=F32)
            * score_scale
        )
        allowed = (sequence_numbers[:, None] == sequence_numbers[None, :]) & (
            local_index[:, None] >= local_index[None, :]
        )
        return jnp.where(allowed, scores, -1e30)

    scores = block_scores()
    row_peak = jnp.max(scores, axis=-1, keepdims=True)
    exp_scores = jnp.exp(scores - row_peak)
    row_total = jnp.sum(exp_scores, axis=-1, keepdims=True)
    probabilities = exp_scores / row_total
    log_totals = row_peak + jnp.log(row_total)
    outputs = jnp.einsum(
        "hgqk,khd->qhgd", probabilities.astype(B16), value_matrix, preferred_element_type=F32
    )
    attended_low = outputs.reshape(tok_count, q_heads * head_dim).astype(B16)
    branch_part = jnp.dot(attended_low, w_out, preferred_element_type=F32).astype(B16)
    branch = scatter_sum(
        lambda z: lax.dynamic_slice_in_dim(branch_part, z * own_rows, own_rows, 0).astype(F32),
        "tensor",
    )
    middle = own(inputs) + branch
    normed_two, pull_two = jax.vjp(rms_norm, middle, moe_gain)
    hidden_rows = normed_two.astype(B16)
    logits = jnp.dot(hidden_rows, w_router, preferred_element_type=F32)
    expert_ids = jnp.arange(experts)
    picked = (own(routes)[:, :, None] == expert_ids[None, None, :]).astype(F32)

    def route_weights(logit_vals):
        probabilities = jax.nn.softmax(logit_vals, axis=-1)
        chosen = jnp.sum(picked * probabilities[:, None, :], axis=-1)
        return chosen / jnp.sum(chosen, axis=-1, keepdims=True)

    weights, pull_router = jax.vjp(route_weights, logits)
    combine = jnp.sum(picked * weights[:, :, None], axis=1)
    high = combine.astype(B16)
    low = (combine - high.astype(F32)).astype(B16)
    spare = -(2 * experts) % 128
    packed_rows = jnp.concatenate(
        [hidden_rows, high, low, jnp.zeros((own_rows, spare), B16)], axis=1
    )
    packed_own = gather_blocks(packed_rows, "tensor", 0)
    packed_of = [packed_own] + [swap(packed_own, "expert", group * r) for r in range(1, rounds)]

    passes = [expert_pass(ids, p, d, gate_up, down, experts) for p, d in zip(packed_of, dy_of)]
    backs = [passes[0][0]] + [swap(passes[r][0], "expert", group * r) for r in range(1, rounds)]

    def sum_rows(parts, z):
        pieces = [
            lax.dynamic_slice_in_dim(p, z * own_rows, own_rows, 0).astype(F32) for p in parts
        ]
        return functools.reduce(jnp.add, pieces)

    back = scatter_sum(lambda z: sum_rows(backs, z), "tensor")

    out_parts = []
    for _, _, act in passes:
        terms = [
            jnp.dot(act[d], down[d], preferred_element_type=F32) for d in range(group)
        ]
        out_parts.append(functools.reduce(jnp.add, terms).astype(B16))
    out_parts = out_parts[:1] + [
        swap(out_parts[r], "expert", group * r) for r in range(1, rounds)
    ]
    mixed = scatter_sum(lambda z: sum_rows(out_parts, z), "tensor")
    block_out = swap_columns((middle + mixed).astype(B16), "tensor")

    held = {}
    for d in reversed(range(group)):
        gu = [tn_dot(p[1][d], packed[:, :model_width]) for p, packed in zip(passes, packed_of)]
        dn = [tn_dot(p[2][d], dy) for p, dy in zip(passes, dy_of)]
        held[d] = (functools.reduce(jnp.add, gu), functools.reduce(jnp.add, dn))
    mask = 1
    while mask < group:
        keep = {}
        for d in sorted(held):
            if d & mask:
                continue
            keep[d] = tuple(
                mine + swap(theirs.astype(B16), "expert", mask).astype(F32)
                for mine, theirs in zip(held[d], held[d ^ mask])
            )
        held = keep
        mask *= 2
    gate_up_grad, down_grad_flat = held[0]
    shape = (local_experts, hidden, model_width)
    gate_grad = jnp.swapaxes(gate_up_grad[:pair].reshape(shape), 1, 2)
    up_grad = jnp.swapaxes(gate_up_grad[pair:].reshape(shape), 1, 2)
    down_grad = down_grad_flat.reshape(shape)

    hidden_grad = back[:, :model_width]
    combine_grad = back[:, model_width : model_width + experts]
    weight_grad = jnp.sum(picked * combine_grad[:, None, :], axis=-1)
    (logit_grad,) = pull_router(weight_grad)
    logit_low = logit_grad.astype(B16)
    router_grad = tn_dot(logit_low, hidden_rows)
    hidden_grad = hidden_grad + nt_dot(logit_low, w_router)
    middle_norm_grad, moe_gain_grad = pull_two(hidden_grad)
    middle_grad = middle_norm_grad + own(dy_own).astype(F32)
    branch_low = gather_blocks(middle_grad.astype(B16), "tensor", 0)

    out_weight_grad = tn_dot(attended_low, branch_low)
    attended_grad = (
        nt_dot(branch_low, w_out).astype(B16).reshape(tok_count, kv_heads, group_size, head_dim)
    )
    scores = block_scores()
    probabilities = jnp.exp(scores - log_totals)
    prob_grad = jnp.einsum(
        "qhgd,khd->hgqk", attended_grad, value_matrix, preferred_element_type=F32
    )
    row_delta = jnp.sum(probabilities * prob_grad, axis=-1, keepdims=True)
    score_low = (probabilities * (prob_grad - row_delta)).astype(B16)
    query_grads = (
        jnp.einsum("hgqk,khd->qhgd", score_low, key_low, preferred_element_type=F32) * score_scale
    )
    key_grad = (
        jnp.einsum("hgqk,qhgd->khd", score_low, query_low, preferred_element_type=F32)
        * score_scale
    )
    value_grad = jnp.einsum(
        "hgqk,qhgd->khd", probabilities.astype(B16), attended_grad, preferred_element_type=F32
    )
    query_pre_grad, query_gain_part = pull_query(query_grads.reshape(tok_count, q_heads, head_dim))
    key_pre_grad, key_gain_part = pull_key(key_grad)
    query_grad_low = query_pre_grad.reshape(tok_count, q_heads * head_dim).astype(B16)
    key_grad_low = key_pre_grad.reshape(tok_count, kv_heads * head_dim).astype(B16)
    value_grad_low = value_grad.reshape(tok_count, kv_heads * head_dim).astype(B16)

    hidden_one = nt_dot(query_grad_low, w_query)
    hidden_one = hidden_one + nt_dot(key_grad_low, key_projection)
    hidden_one = hidden_one + nt_dot(value_grad_low, value_projection)
    scale = lax.rsqrt(jnp.mean(inputs * inputs, axis=-1, keepdims=True) + 1e-06)
    gained = hidden_one * attn_gain
    along_part = jnp.sum(gained * inputs, axis=-1)
    attn_gain_part = jnp.sum(hidden_one * (inputs * scale), axis=0)
    along = sum_everywhere(along_part, "tensor")
    hidden_one_low = hidden_one.astype(B16)
    width = model_width // tensor_size

    def columns(values, z):
        return lax.dynamic_slice_in_dim(values, z * width, width, values.ndim - 1)

    hidden_one_cols = scatter_sum(lambda z: columns(hidden_one_low, z).astype(F32), "tensor")
    gain_cols = columns(attn_gain, tensor_pos)
    input_cols = columns(inputs, tensor_pos)
    input_grad = columns(branch_low, tensor_pos).astype(F32) + scale * (
        hidden_one_cols * gain_cols
        - input_cols * (scale * scale * (along / model_width)[:, None])
    )
    query_weight_grad = tn_dot(first_hidden, query_grad_low)
    key_weight_grad = tn_dot(first_hidden, key_grad_low)
    value_weight_grad = tn_dot(first_hidden, value_grad_low)

    def over_experts(values, dim):
        return lax.psum_scatter(
            values.astype(B16), "expert", scatter_dimension=dim, tiled=True
        ).astype(F32)

    def share_of_sum(values):
        total = sum_everywhere(sum_everywhere(values, "tensor"), "expert")
        size = total.shape[-1] // expert_size
        return lax.dynamic_slice_in_dim(total, expert_pos * size, size, total.ndim - 1)

    router_and_gain = share_of_sum(jnp.concatenate([router_grad, moe_gain_grad[None]], axis=0))
    attn_gain_grad = share_of_sum(attn_gain_part)
    head_gains = share_of_sum(jnp.stack([query_gain_part, key_gain_part]))
    return (
        block_out,
        input_grad,
        attn_gain_grad,
        over_experts(query_weight_grad, 0),
        over_experts(key_weight_grad, 0),
        over_experts(value_weight_grad, 0),
        head_gains[0],
        head_gains[1],
        over_experts(out_weight_grad, 1),
        router_and_gain[experts],
        jnp.swapaxes(router_and_gain[:experts], 0, 1),
        gate_grad,
        up_grad,
        down_grad,
    )


def solution(mesh):
    placed = (
        P("expert", None),
        P("expert"),
        P("expert", None),
        P(),
        P(None, "tensor"),
        P(None, "tensor"),
        P(None, "tensor"),
        P(),
        P(),
        P("tensor", None),
        P(),
        P(),
        P("expert", None, "tensor"),
        P("expert", None, "tensor"),
        P("expert", "tensor", None),
        P("expert", "tensor"),
    )
    return jax.shard_map(
        per_device,
        mesh=mesh,
        in_specs=placed,
        out_specs=(
            P("expert", "tensor"),
            P("expert", "tensor"),
            P("expert"),
            P("expert", "tensor"),
            P("expert", "tensor"),
            P("expert", "tensor"),
            P("expert"),
            P("expert"),
            P("tensor", "expert"),
            P("expert"),
            P("expert", None),
            P("expert", None, "tensor"),
            P("expert", None, "tensor"),
            P("expert", "tensor", None),
        ),
        check_vma=False,
    )
```

```python
import functools

import jax
import jax.numpy as jnp
import ml_dtypes
import numpy as np
from jax import lax
from jax.experimental import pallas as pl
from jax.experimental.pallas import tpu as pltpu
from jax.sharding import PartitionSpec as P

F32 = jnp.float32
B16 = jnp.bfloat16
EPS = 1e-06


def swap(values, axis, mask):
    count = lax.axis_size(axis)
    return lax.ppermute(values, axis, [(i, i ^ mask) for i in range(count)])


def bits_of(axis):
    return lax.axis_size(axis).bit_length() - 1


def gather_pieces(block, axis):
    held = {0: block}
    for bit in reversed(range(bits_of(axis))):
        mask = 1 << bit
        held.update({d ^ mask: swap(v, axis, mask) for d, v in list(held.items())})
    return [held[d] for d in range(lax.axis_size(axis))]


def gather_columns(block, axis):
    me = lax.axis_index(axis)
    size = block.shape[1]
    whole = jnp.zeros((block.shape[0], size * lax.axis_size(axis)), block.dtype)
    for d, v in enumerate(gather_pieces(block, axis)):
        whole = lax.dynamic_update_slice_in_dim(whole, v, (me ^ d) * size, 1)
    return whole


def scatter_terms(pieces, axis):
    return [pieces[0]] + scatter_terms_of(pieces, axis)


def scatter_terms_of(pieces, axis):
    held = {d: v for d, v in enumerate(pieces)}
    terms = []
    for bit in range(bits_of(axis)):
        mask = 1 << bit
        came = {d: swap(held[d ^ mask], axis, mask) for d in held if not d & mask}
        terms.append(came[0])
        held = {d: add_low(held[d], v) if d else None for d, v in came.items()}
    return terms


def after(values, *others):
    return lax.optimization_barrier((values, others))[0]


def add_low(*values):
    return functools.reduce(jnp.add, [v.astype(F32) for v in values]).astype(B16)


def swap_columns(rows, axis):
    count = lax.axis_size(axis)
    me = lax.axis_index(axis)
    height, width = rows.shape[0], rows.shape[1] // count
    whole = jnp.zeros((height * count, width), rows.dtype)
    for d in range(count):
        piece = lax.dynamic_slice_in_dim(rows, (me ^ d) * width, width, 1)
        if d:
            piece = swap(piece, axis, d)
        whole = lax.dynamic_update_slice_in_dim(whole, piece, (me ^ d) * height, 0)
    return whole


def sum_everywhere(values, axis):
    for bit in range(bits_of(axis)):
        values = values + swap(values, axis, 1 << bit)
    return values


def nn_dot(left, right):
    return jnp.dot(left, right, preferred_element_type=F32)


def nt_dot(left, right):
    return lax.dot_general(left, right, (((1,), (1,)), ((), ())), preferred_element_type=F32)


def tn_dot(left, right):
    return lax.dot_general(left, right, (((0,), (0,)), ((), ())), preferred_element_type=F32)


def vmem(*count):
    return [pl.BlockSpec(memory_space=pltpu.VMEM) for _ in range(count[0])]


def hbm(count):
    return [pl.BlockSpec(memory_space=pl.ANY) for _ in range(count)]


SMEM_SPEC = pl.BlockSpec(memory_space=pltpu.SMEM)


def params(mib=56):
    return pltpu.CompilerParams(vmem_limit_bytes=mib << 20)


def cost():
    return pl.CostEstimate(flops=1 << 20, bytes_accessed=1 << 16, transcendentals=0)


def shaped(shape, dtype):
    return jax.ShapeDtypeStruct(shape, dtype)


def rope_table(length, head_dim):
    half = head_dim // 2
    frequency = np.power(1000000.0, -2.0 * np.arange(half, dtype=np.float32) / head_dim)
    angles = np.arange(length, dtype=np.float32)[:, None] * frequency.astype(np.float32)[None, :]
    angles = angles.astype(np.float64)
    rest = np.concatenate(
        [np.cos(angles), np.cos(angles), -np.sin(angles), np.sin(angles)], axis=1
    )
    terms = []
    for _ in range(3):
        term = rest.astype(np.float32).astype(ml_dtypes.bfloat16)
        terms.append(term)
        rest = rest - term.astype(np.float64)
    return np.concatenate(terms, axis=1)


def norm_scale(values):
    return lax.rsqrt(jnp.mean(values * values, axis=-1, keepdims=True) + EPS)


def turned(values, cos, sine):
    return values * cos + pltpu.roll(values, values.shape[-1] // 2, 1) * sine


def turned_back(grads, cos, sine):
    return grads * cos + pltpu.roll(grads * sine, grads.shape[-1] // 2, 1)


def forward_kernel(
    tile, z_ref,
    seq_col, seq_row, table, x, gain, wk, wv, q_gain, k_gain, wq, wo,
    *refs,
):
    pieces, refs = refs[:-11], refs[-11:]
    h1, q_pre, q_low, k_pre, k_low, v_low, att, lse, turns, bias, acc = refs
    step = pl.program_id(0)
    rows = x.shape[0]
    head = wk.shape[1]
    per_step = wq.shape[1] // head

    @pl.when(step == 0)
    def _():
        values = x[...].astype(F32)
        h1[...] = (values * norm_scale(values) * gain[...]).astype(B16)
        query = lax.broadcasted_iota(jnp.int32, (rows, rows), 0)
        key = lax.broadcasted_iota(jnp.int32, (rows, rows), 1)
        same = seq_col[...] == seq_row[...]
        position = jnp.sum(jnp.where(same & (key < query), 1.0, 0.0), axis=1, keepdims=True)
        bias[...] = jnp.where(same & (key <= query), 0.0, -1e30)
        chosen = jnp.where(key == position.astype(jnp.int32), 1.0, 0.0).astype(B16)
        three = nn_dot(chosen, table[...])
        wide = 2 * head
        turns[...] = three[:, :wide] + three[:, wide : 2 * wide] + three[:, 2 * wide :]
        keys = nn_dot(h1[...], wk[...])
        k_pre[...] = keys
        k_low[...] = turned(
            keys * norm_scale(keys) * k_gain[...], turns[:, :head], turns[:, head:]
        ).astype(B16)
        v_low[...] = nn_dot(h1[...], wv[...]).astype(B16)
        lse[...] = jnp.zeros_like(lse)
        acc[...] = jnp.zeros_like(acc)

    queries = nn_dot(h1[...], wq[...])
    q_pre[...] = queries
    lane = lax.broadcasted_iota(jnp.int32, (tile, lse.shape[1]), 1)
    for i in range(per_step):
        at = slice(i * head, (i + 1) * head)
        mine = queries[:, at]
        q_low[:, at] = turned(
            mine * norm_scale(mine) * q_gain[...], turns[:, :head], turns[:, head:]
        ).astype(B16)
        for t in range(rows // tile):
            band = slice(t * tile, (t + 1) * tile)
            seen = (t + 1) * tile
            scores = nt_dot(q_low[band, at], k_low[:seen, :]) * head ** (-0.5) + bias[band, :seen]
            peak = jnp.max(scores, axis=1, keepdims=True)
            shares = jnp.exp(scores - peak)
            total = jnp.sum(shares, axis=1, keepdims=True)
            att[band, at] = nn_dot((shares / total).astype(B16), v_low[:seen, :]).astype(B16)
            lse[band, :] += jnp.where(lane == step * per_step + i, peak + jnp.log(total), 0.0)
    acc[...] += nn_dot(att[...], wo[...])

    @pl.when(step == pl.num_programs(0) - 1)
    def _():
        size = pieces[0].shape[0]
        for d, piece in enumerate(pieces):
            piece[...] = acc[pl.ds(pl.multiple_of((z_ref[0] ^ d) * size, size), size), :].astype(B16)


def attention_forward(z, seq, x, gain, wq, wk, wv, q_gain, k_gain, wo, parts):
    rows, width = x.shape
    head = wk.shape[1]
    block = min(2 * head, wq.shape[1])
    steps = wq.shape[1] // block
    table = jnp.asarray(rope_table(rows, head))
    whole = lambda *shape: pl.BlockSpec(shape, lambda g, z: (0,) * len(shape))
    column = lambda height: pl.BlockSpec((height, block), lambda g, z: (0, g))
    own = rows // parts
    outs = [shaped((own, width), B16)] * parts + [
        shaped((rows, width), B16),
        shaped((rows, wq.shape[1]), F32),
        shaped((rows, wq.shape[1]), B16),
        shaped((rows, head), F32),
        shaped((rows, head), B16),
        shaped((rows, head), B16),
        shaped((rows, wq.shape[1]), B16),
        shaped((rows, 128), F32),
        shaped((rows, 2 * head), F32),
    ]
    out = pl.pallas_call(
        functools.partial(forward_kernel, min(rows, 256)),
        grid_spec=pltpu.PrefetchScalarGridSpec(
            num_scalar_prefetch=1,
            grid=(steps,),
            in_specs=[
                whole(rows, 1), whole(1, rows), whole(*table.shape), whole(rows, width),
                whole(1, width), whole(width, head), whole(width, head), whole(1, head),
                whole(1, head), column(width), pl.BlockSpec((block, width), lambda g, z: (g, 0)),
            ],
            out_specs=[whole(own, width)] * parts + [
                whole(rows, width), column(rows), column(rows), whole(rows, head),
                whole(rows, head), whole(rows, head), column(rows), whole(rows, 128),
                whole(rows, 2 * head),
            ],
            scratch_shapes=[pltpu.VMEM((rows, rows), F32), pltpu.VMEM((rows, width), F32)],
        ),
        out_shape=outs,
        compiler_params=params(),
        cost_estimate=cost(),
    )(
        z, seq.reshape(rows, 1), seq.reshape(1, rows), table, x, gain.reshape(1, width),
        wk, wv, q_gain.reshape(1, head), k_gain.reshape(1, head), wq, wo,
    )
    return out[:parts], out[parts:]


def norm_back(grads, values, gain):
    scale = norm_scale(values)
    unit = values * scale
    gained = grads * gain
    back = scale * (gained - unit * jnp.mean(gained * unit, axis=-1, keepdims=True))
    return back, jnp.sum(grads * unit, axis=0, keepdims=True)


def backward_kernel(
    tile, parts, z_ref,
    seq_col, seq_row, x, gain, wk, wv, q_gain, k_gain, wq, wo,
    q_pre, q_low, k_pre, k_low, v_low, lse, turns, *refs,
):
    came, refs = refs[:parts], refs[parts:]
    cols, refs = refs[:parts], refs[parts:]
    branch, low, along, gains, bias, acc, dkey, dvalue = refs
    step = pl.program_id(0)
    last = pl.num_programs(0) - 1
    rows, width = x.shape
    head = wk.shape[1]
    per_step = wq.shape[1] // head
    cos, sine = turns[:, :head], turns[:, head:]

    @pl.when(step == 0)
    def _():
        size = came[0].shape[0]
        for d, piece in enumerate(came):
            branch[pl.ds(pl.multiple_of((z_ref[0] ^ d) * size, size), size), :] = piece[...]
        query = lax.broadcasted_iota(jnp.int32, (rows, rows), 0)
        key = lax.broadcasted_iota(jnp.int32, (rows, rows), 1)
        same = seq_col[...] == seq_row[...]
        bias[...] = jnp.where(same & (key <= query), 0.0, -1e30)
        acc[...] = jnp.zeros_like(acc)
        dkey[...] = jnp.zeros_like(dkey)
        dvalue[...] = jnp.zeros_like(dvalue)
        gains[...] = jnp.zeros_like(gains)

    @pl.when(step < last)
    def _():
        datt = nt_dot(branch[...], wo[...]).astype(B16)
        lane = lax.broadcasted_iota(jnp.int32, (tile, lse.shape[1]), 1)
        for i in range(per_step):
            at = slice(i * head, (i + 1) * head)
            parts_q = []
            for t in range(rows // tile):
                band = slice(t * tile, (t + 1) * tile)
                seen = (t + 1) * tile
                logsum = jnp.sum(
                    jnp.where(lane == step * per_step + i, lse[band, :], 0.0),
                    axis=1, keepdims=True,
                )
                scores = (
                    nt_dot(q_low[band, at], k_low[:seen, :]) * head ** (-0.5) + bias[band, :seen]
                )
                p = jnp.exp(scores - logsum)
                dout = datt[band, at]
                dp = nt_dot(dout, v_low[:seen, :])
                delta = jnp.sum(p * dp, axis=1, keepdims=True)
                ds = (p * (dp - delta)).astype(B16)
                parts_q.append(nn_dot(ds, k_low[:seen, :]) * head ** (-0.5))
                dkey[:seen, :] += tn_dot(ds, q_low[band, at]) * head ** (-0.5)
                dvalue[:seen, :] += tn_dot(p.astype(B16), dout)
            dq = turned_back(jnp.concatenate(parts_q, axis=0), cos, sine)
            back, gain_part = norm_back(dq, q_pre[:, at], q_gain[...])
            low[:, at] = back.astype(B16)
            gains[1:2, :head] += gain_part
        acc[...] += nt_dot(low[...], wq[...])

    @pl.when(step == last)
    def _():
        dk = turned_back(dkey[...], cos, sine)
        back, gain_part = norm_back(dk, k_pre[...], k_gain[...])
        gains[2:3, :head] = gain_part
        low[:, :head] = back.astype(B16)
        low[:, head : 2 * head] = dvalue[...].astype(B16)
        acc[...] += nt_dot(low[:, :head], wk[...]) + nt_dot(low[:, head : 2 * head], wv[...])
        values = x[...].astype(F32)
        total = acc[...]
        along[...] = jnp.sum(total * gain[...] * values, axis=1, keepdims=True)
        gains[0:1, :] = jnp.sum(total * (values * norm_scale(values)), axis=0, keepdims=True)
        size = cols[0].shape[1]
        for d, piece in enumerate(cols):
            piece[...] = acc[:, pl.ds(pl.multiple_of((z_ref[0] ^ d) * size, size), size)].astype(B16)


def attention_backward(z, seq, x, gain, wq, wk, wv, q_gain, k_gain, wo, kept, came):
    rows, width = x.shape
    head = wk.shape[1]
    block = 2 * head
    steps = wq.shape[1] // block
    parts = len(came)
    q_pre, q_low, k_pre, k_low, v_low, lse, turns = kept
    whole = lambda *shape: pl.BlockSpec(shape, lambda g, z: (0,) * len(shape))
    column = lambda height: pl.BlockSpec(
        (height, block), lambda g, z: (0, jnp.minimum(g, steps - 1))
    )
    outs = [shaped((rows, width // parts), B16)] * parts + [
        shaped((rows, width), B16),
        shaped((rows, block * (steps + 1)), B16),
        shaped((rows, 1), F32),
        shaped((8, width), F32),
    ]
    out = pl.pallas_call(
        functools.partial(backward_kernel, min(rows, 256), parts),
        grid_spec=pltpu.PrefetchScalarGridSpec(
            num_scalar_prefetch=1,
            grid=(steps + 1,),
            in_specs=[
                whole(rows, 1), whole(1, rows), whole(rows, width), whole(1, width),
                whole(width, head), whole(width, head), whole(1, head), whole(1, head),
                column(width),
                pl.BlockSpec((block, width), lambda g, z: (jnp.minimum(g, steps - 1), 0)),
                column(rows), column(rows), whole(rows, head), whole(rows, head),
                whole(rows, head), whole(rows, 128), whole(rows, 2 * head),
            ] + [whole(rows // parts, width)] * parts,
            out_specs=[whole(rows, width // parts)] * parts + [
                whole(rows, width),
                pl.BlockSpec((rows, block), lambda g, z: (0, g)),
                whole(rows, 1),
                whole(8, width),
            ],
            scratch_shapes=[
                pltpu.VMEM((rows, rows), F32), pltpu.VMEM((rows, width), F32),
                pltpu.VMEM((rows, head), F32), pltpu.VMEM((rows, head), F32),
            ],
        ),
        out_shape=outs,
        compiler_params=params(),
        cost_estimate=cost(),
    )(
        z, seq.reshape(rows, 1), seq.reshape(1, rows), x, gain.reshape(1, width), wk, wv,
        q_gain.reshape(1, head), k_gain.reshape(1, head), wq, wo,
        q_pre, q_low, k_pre, k_low, v_low, lse, turns, *came,
    )
    return out[:parts], out[parts:]


def router_kernel(terms, experts, *refs):
    parts, (x, routes, gain, router, middle, packed, shares) = refs[:terms], refs[terms:]
    total = x[...].astype(F32)
    branch = parts[0][...].astype(F32)
    for part in parts[1:]:
        branch = branch + part[...].astype(F32)
    total = total + branch
    middle[...] = total
    width = total.shape[1]
    hidden = (total * norm_scale(total) * gain[...]).astype(B16)
    packed[:, :width] = hidden
    logits = nt_dot(hidden, router[...])
    lane = lax.broadcasted_iota(jnp.int32, logits.shape, 1)
    twin = jnp.where(lane < experts, lane, lane - experts)
    chosen = jnp.zeros(logits.shape, jnp.bool_)
    for k in range(routes.shape[1]):
        chosen = chosen | (twin == routes[:, k : k + 1])
    chosen = chosen & (lane < 2 * experts)
    peak = jnp.max(jnp.where(chosen, logits, -1e30), axis=1, keepdims=True)
    raised = jnp.where(chosen, jnp.exp(jnp.minimum(logits - peak, 0.0)), 0.0)
    share = raised / jnp.sum(jnp.where(lane < experts, raised, 0.0), axis=1, keepdims=True)
    shares[...] = share
    high = share.astype(B16).astype(F32)
    packed[:, width:] = jnp.where(lane < experts, high, share - high).astype(B16)


def row_block(height, width):
    return pl.BlockSpec((height, width), lambda g, z: (z[0], 0))


def route_rows(z, terms, x, routes, gain, router, experts):
    own, width = terms[0].shape
    extra = router.shape[0]
    whole = lambda *shape: pl.BlockSpec(shape, lambda g, z: (0,) * len(shape))
    count = len(terms)

    def kernel(z_ref, *refs):
        router_kernel(count, experts, *refs)

    return pl.pallas_call(
        kernel,
        grid_spec=pltpu.PrefetchScalarGridSpec(
            num_scalar_prefetch=1,
            grid=(1,),
            in_specs=[whole(own, width)] * count + [
                row_block(own, width), row_block(own, routes.shape[1]), whole(1, width),
                whole(extra, width),
            ],
            out_specs=[whole(own, width), whole(own, width + extra), whole(own, extra)],
        ),
        out_shape=[
            shaped((own, width), F32), shaped((own, width + extra), B16), shaped((own, extra), F32),
        ],
        compiler_params=params(),
        cost_estimate=cost(),
    )(z, *terms, x, routes, gain.reshape(1, width), router)


def rows_back_kernel(count, experts, *refs):
    terms, (dy, middle, shares, gain, router, dbranch, sums) = refs[:count], refs[count:]
    width = middle.shape[1]
    total = terms[0][...].astype(F32)
    for term in terms[1:]:
        total = total + term[...].astype(F32)
    values = middle[...]
    share = shares[...]
    lane = lax.broadcasted_iota(jnp.int32, share.shape, 1)
    dshare = total[:, width:]
    share = jnp.where(lane < experts, share, 0.0)
    mean = jnp.sum(share * dshare, axis=1, keepdims=True)
    dlogits = (share * (dshare - mean)).astype(B16)
    scale = norm_scale(values)
    unit = values * scale
    hidden = (unit * gain[...]).astype(B16)
    dhidden = total[:, :width] + nn_dot(dlogits, router[...])
    gained = dhidden * gain[...]
    back = scale * (gained - unit * jnp.mean(gained * unit, axis=-1, keepdims=True))
    dbranch[...] = (back + dy[...].astype(F32)).astype(B16)
    grads = tn_dot(dlogits, hidden)
    sums[:experts, :] = grads[:experts, :]
    sums[experts:, :] = jnp.broadcast_to(
        jnp.sum(dhidden * unit, axis=0, keepdims=True), (8, width)
    )


def rows_back(z, terms, dy, middle, shares, gain, router, experts):
    own, width = middle.shape
    extra = router.shape[0]
    whole = lambda *shape: pl.BlockSpec(shape, lambda g, z: (0,) * len(shape))
    count = len(terms)

    def kernel(z_ref, *refs):
        rows_back_kernel(count, experts, *refs)

    return pl.pallas_call(
        kernel,
        grid_spec=pltpu.PrefetchScalarGridSpec(
            num_scalar_prefetch=1,
            grid=(1,),
            in_specs=[whole(own, width + extra)] * count + [
                row_block(own, width), whole(own, width), whole(own, extra), whole(1, width),
                whole(extra, width),
            ],
            out_specs=[whole(own, width), whole(experts + 8, width)],
        ),
        out_shape=[shaped((own, width), B16), shaped((experts + 8, width), F32)],
        compiler_params=params(),
        cost_estimate=cost(),
    )(z, *terms, dy, middle, shares, gain.reshape(1, width), router)


def expert_kernel(parts, group, slots, hidden, experts, *refs):
    z_ref, ids_ref, refs = refs[0], refs[1], refs[2:]
    packed, refs = refs[:parts], refs[parts:]
    dy, refs = refs[0], refs[1:]
    weights, refs = refs[: 2 * group], refs[2 * group :]
    backs, refs = refs[:parts], refs[parts:]
    held, dgu_out, act_out, gate_up, down, dgu_buf, act_buf, total, sems, out_sems = refs
    rows, width = dy.shape
    pair = 2 * hidden

    def fetch(d):
        slot = d % slots
        return [
            pltpu.make_async_copy(weights[2 * d], gate_up.at[slot], sems.at[0, slot]),
            pltpu.make_async_copy(weights[2 * d + 1], down.at[slot], sems.at[1, slot]),
        ]

    def store(d):
        return [
            pltpu.make_async_copy(dgu_buf.at[d % 2], dgu_out.at[d], out_sems.at[0, d % 2]),
            pltpu.make_async_copy(act_buf.at[d % 2], act_out.at[d], out_sems.at[1, d % 2]),
        ]

    for d in range(min(slots, group)):
        for copy in fetch(d):
            copy.start()
    size = packed[0].shape[0]
    extra = packed[0].shape[1] - width

    def rows_of(d):
        return pl.ds(pl.multiple_of((z_ref[0] ^ d) * size, size), size)

    for d in range(parts):
        held[rows_of(d), :] = packed[d][...]
    shares = held[:, width:].astype(F32)
    lane = lax.broadcasted_iota(jnp.int32, (rows, extra), 1)
    first = lax.broadcasted_iota(jnp.int32, (rows, pair), 1) < hidden

    def share_of(expert):
        mine = (lane == expert) | (lane == expert + experts)
        return jnp.sum(jnp.where(mine, shares, 0.0), axis=1, keepdims=True)

    dshares = jnp.zeros((rows, extra), F32)
    for d in range(group):
        slot = d % slots
        for copy in fetch(d):
            copy.wait()
        id_a, id_b = ids_ref[2 * d], ids_ref[2 * d + 1]
        both = nt_dot(held[:, :width], gate_up[slot])
        raw = nt_dot(dy[...], down[slot])
        gate, up = both[:, :pair], both[:, pair:]
        share = jnp.where(first, share_of(id_a), share_of(id_b))
        sig = 1.0 / (1.0 + jnp.exp(-gate))
        silu = gate * sig
        act = (silu * up).astype(B16).astype(F32)
        product = act * raw
        part_a = jnp.sum(jnp.where(first, product, 0.0), axis=1, keepdims=True)
        part_b = jnp.sum(jnp.where(first, 0.0, product), axis=1, keepdims=True)
        dshares = dshares + jnp.where(lane == id_a, part_a, 0.0)
        dshares = dshares + jnp.where(lane == id_b, part_b, 0.0)
        dact = share * raw
        dgate = dact * up * (sig * (1.0 + gate * (1.0 - sig)))
        dup = dact * silu
        if d >= 2:
            for copy in store(d - 2):
                copy.wait()
        dgu_buf[d % 2, :, :pair] = dgate.astype(B16)
        dgu_buf[d % 2, :, pair:] = dup.astype(B16)
        act_buf[d % 2] = (share * act).astype(B16)
        for copy in store(d):
            copy.start()
        term = nn_dot(dgu_buf[d % 2], gate_up[slot])
        total[...] = term if d == 0 else total[...] + term
        if d + slots < group:
            for copy in fetch(d + slots):
                copy.start()
    for d in range(parts):
        backs[d][:, :width] = total[rows_of(d), :].astype(B16)
    held_share = dshares.astype(B16)
    total[:, :extra] = held_share.astype(F32)
    for d in range(parts):
        backs[d][:, width:] = total[rows_of(d), :extra].astype(B16)
    for d in range(max(0, group - 2), group):
        for copy in store(d):
            copy.wait()


def expert_pass(z, ids, packed, dy, weights, experts):
    rows, width = dy.shape
    parts = len(packed)
    size, full = packed[0].shape
    group = len(weights)
    pair = weights[0][1].shape[0]
    slots = min(group, 4)
    out = pl.pallas_call(
        functools.partial(expert_kernel, parts, group, slots, pair // 2, experts),
        in_specs=[SMEM_SPEC, SMEM_SPEC] + vmem(parts + 1) + hbm(2 * group),
        out_specs=vmem(parts + 1) + hbm(2),
        out_shape=[shaped((size, full), B16)] * parts + [
            shaped((rows, full), B16),
            shaped((group, rows, 2 * pair), B16),
            shaped((group, rows, pair), B16),
        ],
        scratch_shapes=[
            pltpu.VMEM((slots, 2 * pair, width), B16),
            pltpu.VMEM((slots, pair, width), B16),
            pltpu.VMEM((2, rows, 2 * pair), B16),
            pltpu.VMEM((2, rows, pair), B16),
            pltpu.VMEM((rows, width), F32),
            pltpu.SemaphoreType.DMA((2, slots)),
            pltpu.SemaphoreType.DMA((2, 2)),
        ],
        compiler_params=params(58),
        cost_estimate=cost(),
    )(z, ids, *packed, dy, *[w for two in weights for w in two])
    return out[:parts], out[parts:]


def outputs_kernel(parts, sources, group, z_ref, *refs):
    acts, refs = refs[:sources], refs[sources:]
    downs, refs = refs[:group], refs[group:]
    outs, total = refs[:-1], refs[-1]
    size = outs[0].shape[0]
    for s in range(sources):
        value = nn_dot(acts[s][0], downs[0][...])
        for d in range(1, group):
            value = value + nn_dot(acts[s][d], downs[d][...])
        total[...] = value
        for d in range(parts):
            at = pl.ds(pl.multiple_of((z_ref[0] ^ d) * size, size), size)
            outs[s * parts + d][...] = total[at, :].astype(B16)


def expert_outputs(z, acts, downs, parts):
    group, rows, pair = acts[0].shape
    width = downs[0].shape[1]
    out = pl.pallas_call(
        functools.partial(outputs_kernel, parts, len(acts), group),
        grid=(1,),
        in_specs=[SMEM_SPEC]
        + [pl.BlockSpec((group, rows, pair), lambda g: (0, 0, 0)) for _ in acts]
        + [pl.BlockSpec((pair, width), lambda g: (0, 0)) for _ in downs],
        out_specs=[pl.BlockSpec((rows // parts, width), lambda g: (0, 0))] * (len(acts) * parts),
        out_shape=[shaped((rows // parts, width), B16)] * (len(acts) * parts),
        scratch_shapes=[pltpu.VMEM((rows, width), F32)],
        compiler_params=params(),
        cost_estimate=cost(),
    )(z, *acts, *downs)
    return [out[s * parts : (s + 1) * parts] for s in range(len(acts))]


def grads_kernel(sources, *refs):
    ins, refs = refs[: 4 * sources], refs[4 * sources :]
    came, out = refs[:-1], refs[-1]
    step = pl.program_id(0)
    width = out.shape[1]

    def write(part):
        total = came[0][...].astype(F32) if came else 0.0
        for s in range(sources):
            held, dy, dgu, act = ins[4 * s : 4 * s + 4]
            if part < 2:
                total = total + tn_dot(dgu[0], held[:, :width])
            else:
                total = total + tn_dot(act[0], dy[...])
        out[...] = total.astype(B16)

    @pl.when(step < 2)
    def _():
        write(0)

    @pl.when(step == 2)
    def _():
        write(2)


def expert_grads(distance, sources, came):
    held, dy, dgu, act = sources[0]
    rows, full = held.shape
    width = dy.shape[1]
    pair = act.shape[2]
    whole = lambda *shape: pl.BlockSpec(shape, lambda g: (0,) * len(shape))
    line = pl.BlockSpec((pair, width), lambda g: (g, 0))
    return pl.pallas_call(
        functools.partial(grads_kernel, len(sources)),
        grid=(3,),
        in_specs=[
            whole(rows, full),
            whole(rows, width),
            pl.BlockSpec((1, rows, pair), lambda g: (distance, 0, jnp.minimum(g, 1))),
            pl.BlockSpec((1, rows, pair), lambda g: (distance, 0, 0)),
        ] * len(sources) + [line] * len(came),
        out_specs=line,
        out_shape=shaped((3 * pair, width), B16),
        compiler_params=params(),
        cost_estimate=cost(),
    )(*[v for source in sources for v in source], *came)


def per_device(
    tokens,
    sequence_numbers,
    routes,
    attn_gain,
    w_query,
    key_projection,
    value_projection,
    query_gain,
    key_gain,
    w_out,
    moe_gain,
    w_router,
    w_gate,
    w_up,
    w_down,
    cotangent,
):
    tok_count, model_width = tokens.shape
    head_dim = query_gain.shape[0]
    tensor_size = lax.axis_size("tensor")
    tensor_pos = lax.axis_index("tensor")
    expert_size = lax.axis_size("expert")
    expert_pos = lax.axis_index("expert")
    local_experts, _, hidden = w_gate.shape
    experts = local_experts * expert_size
    pair = local_experts * hidden
    group = 2 << ((expert_size // 2).bit_length() // 2)
    rounds = expert_size // group
    z = tensor_pos.astype(jnp.int32).reshape(1)

    gate_up = {
        0: jnp.concatenate(
            [
                jnp.swapaxes(w_gate, 1, 2).reshape(pair, model_width),
                jnp.swapaxes(w_up, 1, 2).reshape(pair, model_width),
            ],
            axis=0,
        )
    }
    down = {0: w_down.reshape(pair, model_width)}
    for bit in reversed(range(1, group.bit_length() - 1)):
        for held in (gate_up, down):
            held.update({d ^ (1 << bit): swap(v, "expert", 1 << bit) for d, v in list(held.items())})
    ids = jnp.concatenate(
        [(expert_pos ^ d) * local_experts + jnp.arange(local_experts) for d in range(group)]
    ).astype(jnp.int32)
    dy_own = lax.all_gather(cotangent, "tensor", axis=1, tiled=True)
    dy_of = [dy_own] + [swap(dy_own, "expert", group * r) for r in range(1, rounds)]

    attention = (
        z, sequence_numbers, tokens, attn_gain, w_query, key_projection, value_projection,
        query_gain, key_gain, w_out,
    )
    branch_parts, kept = attention_forward(*attention, tensor_size)
    first_hidden, attended_low = kept[0], kept[6]
    kept = kept[1:6] + kept[7:]
    terms = scatter_terms(branch_parts, "tensor")

    router_rows = jnp.swapaxes(w_router, 0, 1)
    spare = -(2 * experts) % 128
    router_rows = jnp.concatenate(
        [router_rows, router_rows, jnp.zeros((spare, model_width), B16)], axis=0
    )
    middle, packed_rows, shares = route_rows(
        z, terms, tokens, routes, moe_gain, router_rows, experts
    )
    gate_up = after(gate_up, packed_rows)
    gate_up.update({d ^ 1: swap(v, "expert", 1) for d, v in list(gate_up.items())})
    packed_own = {0: packed_rows}
    packed_of = [{0: swap(packed_rows, "expert", group * r)} for r in range(1, rounds)]
    for bit in reversed(range(bits_of("tensor"))):
        came = {d ^ (1 << bit): swap(v, "tensor", 1 << bit) for d, v in packed_own.items()}
        came = after(came, packed_of)
        packed_own.update(came)
        for r in range(1, rounds):
            packed_of[r - 1].update({d: swap(v, "expert", group * r) for d, v in came.items()})
    down = after(down, packed_own)
    down.update({d ^ 1: swap(v, "expert", 1) for d, v in list(down.items())})
    weights = [(gate_up[d], down[d]) for d in range(group)]
    packed_of = [[p[d] for d in range(tensor_size)] for p in [packed_own] + packed_of]
    passes = [expert_pass(z, ids, p, d, weights, experts) for p, d in zip(packed_of, dy_of)]
    back_parts = [passes[0][0]] + [
        [swap(v, "expert", group * r) for v in passes[r][0]] for r in range(1, rounds)
    ]
    joined = [add_low(*several) for several in zip(*back_parts)]
    joined[0] = None
    back_terms = [part[0] for part in back_parts] + scatter_terms_of(joined, "tensor")

    sources = [(p[1][0], dy, p[1][1], p[1][2]) for p, dy in zip(passes, dy_of)]
    odd = {d: expert_grads(d, sources, ()) for d in range(group - 1, 0, -2)}
    odd = {d: swap(v, "expert", 1) for d, v in odd.items()}
    sums = {d: expert_grads(d, sources, (odd[d + 1],)) for d in range(group - 2, -1, -2)}
    local_sums = list(sums.values())
    mask = 2
    while mask < group:
        came = {d: swap(sums[d ^ mask], "expert", mask) for d in sums if not d & mask}
        sums = {
            d: sums[d].astype(F32) + v.astype(F32) if mask * 2 == group else add_low(sums[d], v)
            for d, v in came.items()
        }
        mask *= 2
    shape = (local_experts, hidden, model_width)
    gate_grad = jnp.swapaxes(sums[0][:pair].reshape(shape), 1, 2)
    up_grad = jnp.swapaxes(sums[0][pair : 2 * pair].reshape(shape), 1, 2)
    down_grad = sums[0][2 * pair :].reshape(shape)

    out_parts = expert_outputs(z, [p[1][2] for p in passes], [w[1] for w in weights], tensor_size)

    back_terms = after(back_terms, local_sums, out_parts)
    dbranch, row_sums = rows_back(
        z, back_terms, dy_own, middle, shares, moe_gain, router_rows, experts
    )
    dbranch_pieces = gather_pieces(dbranch, "tensor")
    branch_low = jnp.zeros((tok_count, model_width), B16)
    for d, v in enumerate(dbranch_pieces):
        at = (tensor_pos ^ d) * v.shape[0]
        branch_low = lax.dynamic_update_slice_in_dim(branch_low, v, at, 0)
    out_grad = tn_dot(attended_low, branch_low).astype(B16)
    dbranch_pieces = after(dbranch_pieces, out_grad)
    col_parts, (_, low, along, gains) = attention_backward(*attention, kept, dbranch_pieces)
    col_terms = scatter_terms(col_parts, "tensor")
    along = sum_everywhere(along, "tensor")
    width = model_width // tensor_size
    inputs = tokens.astype(F32)
    scale = lax.rsqrt(jnp.mean(inputs * inputs, axis=-1, keepdims=True) + EPS)

    def columns(values):
        return lax.dynamic_slice_in_dim(values, tensor_pos * width, width, values.ndim - 1)

    cols = functools.reduce(jnp.add, [t.astype(F32) for t in col_terms])
    input_grad = columns(branch_low).astype(F32) + scale * (
        cols * columns(attn_gain)
        - columns(inputs) * (scale * scale * (along * (1.0 / model_width)))
    )

    out_parts = after(out_parts, dbranch_pieces)
    out_parts = out_parts[:1] + [
        [swap(v, "expert", group * r) for v in out_parts[r]] for r in range(1, rounds)
    ]
    joined = [add_low(*several) for several in zip(*out_parts)]
    joined[0] = None
    out_terms = [part[0] for part in out_parts] + scatter_terms_of(joined, "tensor")
    mixed = functools.reduce(jnp.add, [t.astype(F32) for t in out_terms])
    block_out = swap_columns((middle + mixed).astype(B16), "tensor")

    def over_experts(values, dim):
        return lax.psum_scatter(
            values.astype(B16), "expert", scatter_dimension=dim, tiled=True
        ).astype(F32)

    out_weight_grad = over_experts(out_grad, 1)
    qkv = over_experts(tn_dot(first_hidden, low), 0)
    q_size = w_query.shape[1]

    columns_each = model_width // expert_size
    head_each = head_dim // expert_size
    spread = jnp.pad(
        gains[1:3, :head_dim].reshape(2, expert_size, head_each),
        ((0, 0), (0, 0), (0, columns_each - head_each)),
    )
    small = jnp.concatenate(
        [row_sums[: experts + 1], gains[:1], spread.reshape(2, model_width)], axis=0
    )
    small = small.reshape((small.shape[0],) + (2,) * bits_of("expert") + (columns_each,))
    for bit in range(bits_of("expert")):
        dim = small.ndim - 2
        mine = (expert_pos >> bit) & 1
        send = lax.dynamic_index_in_dim(small, 1 - mine, dim, False)
        keep = lax.dynamic_index_in_dim(small, mine, dim, False)
        small = keep + swap(send, "expert", 1 << bit)
    small = sum_everywhere(small, "tensor")

    return (
        block_out,
        input_grad,
        small[experts + 1],
        qkv[:, :q_size],
        qkv[:, q_size : q_size + head_dim],
        qkv[:, q_size + head_dim :],
        small[experts + 2, :head_each],
        small[experts + 3, :head_each],
        out_weight_grad,
        small[experts],
        jnp.swapaxes(small[:experts], 0, 1),
        gate_grad,
        up_grad,
        down_grad,
    )


def solution(mesh):
    placed = (
        P("expert", None),
        P("expert"),
        P("expert", None),
        P(),
        P(None, "tensor"),
        P(None, "tensor"),
        P(None, "tensor"),
        P(),
        P(),
        P("tensor", None),
        P(),
        P(),
        P("expert", None, "tensor"),
        P("expert", None, "tensor"),
        P("expert", "tensor", None),
        P("expert", "tensor"),
    )
    return jax.shard_map(
        per_device,
        mesh=mesh,
        in_specs=placed,
        out_specs=(
            P("expert", "tensor"),
            P("expert", "tensor"),
            P("expert"),
            P("expert", "tensor"),
            P("expert", "tensor"),
            P("expert", "tensor"),
            P("expert"),
            P("expert"),
            P("tensor", "expert"),
            P("expert"),
            P("expert", None),
            P("expert", None, "tensor"),
            P("expert", None, "tensor"),
            P("expert", "tensor", None),
        ),
        check_vma=False,
    )
```

```python
import functools

import jax
import jax.numpy as jnp
import ml_dtypes
import numpy as np
from jax import lax
from jax.experimental import pallas as pl
from jax.experimental.pallas import tpu as pltpu
from jax.sharding import PartitionSpec as P

F32 = jnp.float32
B16 = jnp.bfloat16
EPS = 1e-06


def swap(values, axis, mask):
    count = lax.axis_size(axis)
    return lax.ppermute(values, axis, [(i, i ^ mask) for i in range(count)])


def bits_of(axis):
    return lax.axis_size(axis).bit_length() - 1


def scatter_terms_of(pieces, axis):
    held = {d: v for d, v in enumerate(pieces)}
    terms = []
    for bit in range(bits_of(axis)):
        mask = 1 << bit
        came = {d: swap(held[d ^ mask], axis, mask) for d in held if not d & mask}
        terms.append(came[0])
        held = {d: add_low(held[d], v) if d else None for d, v in came.items()}
    return terms


def after(values, *others):
    return lax.optimization_barrier((values, others))[0]


def further_terms(pieces, came, axis):
    return passed_on({d: add_low(pieces[d], v) if d else None for d, v in came.items()}, axis)


def passed_on(held, axis):
    terms = []
    for bit in range(1, bits_of(axis)):
        mask = 1 << bit
        came = {d: swap(held[d ^ mask], axis, mask) for d in held if not d & mask}
        terms.append(came[0])
        held = {d: add_low(held[d], v) if d else None for d, v in came.items()}
    return terms


def exchange_near(pieces, axis):
    return {d: swap(pieces[d ^ 1], axis, 1) for d in range(lax.axis_size(axis) - 2, -1, -2)}


def together(*values):
    return lax.optimization_barrier(values)


def add_low(*values):
    return functools.reduce(jnp.add, [v.astype(F32) for v in values]).astype(B16)


def sum_everywhere(values, axis):
    for bit in range(bits_of(axis)):
        values = values + swap(values, axis, 1 << bit)
    return values


def nn_dot(left, right):
    return jnp.dot(left, right, preferred_element_type=F32)


def nt_dot(left, right):
    return lax.dot_general(left, right, (((1,), (1,)), ((), ())), preferred_element_type=F32)


def tn_dot(left, right):
    return lax.dot_general(left, right, (((0,), (0,)), ((), ())), preferred_element_type=F32)


def vmem(*count):
    return [pl.BlockSpec(memory_space=pltpu.VMEM) for _ in range(count[0])]


def hbm(count):
    return [pl.BlockSpec(memory_space=pl.ANY) for _ in range(count)]


SMEM_SPEC = pl.BlockSpec(memory_space=pltpu.SMEM)


def params(mib=56):
    return pltpu.CompilerParams(vmem_limit_bytes=mib << 20)


PACE = 3.0


def cost(micros):
    moved = int(micros * PACE * 3.6e6)
    return pl.CostEstimate(flops=0, bytes_accessed=moved, transcendentals=0)


def shaped(shape, dtype):
    return jax.ShapeDtypeStruct(shape, dtype)


def rope_table(length, head_dim):
    half = head_dim // 2
    frequency = np.power(1000000.0, -2.0 * np.arange(half, dtype=np.float32) / head_dim)
    angles = np.arange(length, dtype=np.float32)[:, None] * frequency.astype(np.float32)[None, :]
    angles = angles.astype(np.float64)
    rest = np.concatenate(
        [np.cos(angles), np.cos(angles), -np.sin(angles), np.sin(angles)], axis=1
    )
    terms = []
    for _ in range(3):
        term = rest.astype(np.float32).astype(ml_dtypes.bfloat16)
        terms.append(term)
        rest = rest - term.astype(np.float64)
    return np.concatenate(terms, axis=1)


def norm_scale(values):
    return lax.rsqrt(jnp.mean(values * values, axis=-1, keepdims=True) + EPS)


def turned(values, cos, sine):
    return values * cos + pltpu.roll(values, values.shape[-1] // 2, 1) * sine


def turned_back(grads, cos, sine):
    return grads * cos + pltpu.roll(grads * sine, grads.shape[-1] // 2, 1)


def forward_kernel(
    tile, z_ref,
    seq_col, seq_row, table, x, gain, wk, wv, q_gain, k_gain, wq, wo,
    *refs,
):
    pieces, refs = refs[:-11], refs[-11:]
    h1, q_pre, q_low, k_pre, k_low, v_low, att, lse, turns, bias, acc = refs
    step = pl.program_id(0)
    rows = x.shape[0]
    head = wk.shape[1]
    per_step = wq.shape[1] // head

    @pl.when(step == 0)
    def _():
        values = x[...].astype(F32)
        h1[...] = (values * norm_scale(values) * gain[...]).astype(B16)
        query = lax.broadcasted_iota(jnp.int32, (rows, rows), 0)
        key = lax.broadcasted_iota(jnp.int32, (rows, rows), 1)
        same = seq_col[...] == seq_row[...]
        position = jnp.sum(jnp.where(same & (key < query), 1.0, 0.0), axis=1, keepdims=True)
        bias[...] = jnp.where(same & (key <= query), 0.0, -1e30)
        chosen = jnp.where(key == position.astype(jnp.int32), 1.0, 0.0).astype(B16)
        three = nn_dot(chosen, table[...])
        wide = 2 * head
        turns[...] = three[:, :wide] + three[:, wide : 2 * wide] + three[:, 2 * wide :]
        keys = nn_dot(h1[...], wk[...])
        k_pre[...] = keys
        k_low[...] = turned(
            keys * norm_scale(keys) * k_gain[...], turns[:, :head], turns[:, head:]
        ).astype(B16)
        v_low[...] = nn_dot(h1[...], wv[...]).astype(B16)
        lse[...] = jnp.zeros_like(lse)
        acc[...] = jnp.zeros_like(acc)

    queries = nn_dot(h1[...], wq[...])
    q_pre[...] = queries
    lane = lax.broadcasted_iota(jnp.int32, (tile, lse.shape[1]), 1)
    for i in range(per_step):
        at = slice(i * head, (i + 1) * head)
        mine = queries[:, at]
        q_low[:, at] = turned(
            mine * norm_scale(mine) * q_gain[...], turns[:, :head], turns[:, head:]
        ).astype(B16)
        for t in range(rows // tile):
            band = slice(t * tile, (t + 1) * tile)
            seen = (t + 1) * tile
            scores = nt_dot(q_low[band, at], k_low[:seen, :]) * head ** (-0.5) + bias[band, :seen]
            peak = jnp.max(scores, axis=1, keepdims=True)
            shares = jnp.exp(scores - peak)
            total = jnp.sum(shares, axis=1, keepdims=True)
            att[band, at] = nn_dot((shares / total).astype(B16), v_low[:seen, :]).astype(B16)
            lse[band, :] += jnp.where(lane == step * per_step + i, peak + jnp.log(total), 0.0)
    acc[...] += nn_dot(att[...], wo[...])

    @pl.when(step == pl.num_programs(0) - 1)
    def _():
        size = pieces[0].shape[0]
        for d, piece in enumerate(pieces):
            piece[...] = acc[pl.ds(pl.multiple_of((z_ref[0] ^ d) * size, size), size), :].astype(B16)


def attention_forward(z, seq, x, gain, wq, wk, wv, q_gain, k_gain, wo, parts):
    rows, width = x.shape
    head = wk.shape[1]
    block = min(2 * head, wq.shape[1])
    steps = wq.shape[1] // block
    table = jnp.asarray(rope_table(rows, head))
    whole = lambda *shape: pl.BlockSpec(shape, lambda g, z: (0,) * len(shape))
    column = lambda height: pl.BlockSpec((height, block), lambda g, z: (0, g))
    own = rows // parts
    outs = [shaped((own, width), B16)] * parts + [
        shaped((rows, width), B16),
        shaped((rows, wq.shape[1]), F32),
        shaped((rows, wq.shape[1]), B16),
        shaped((rows, head), F32),
        shaped((rows, head), B16),
        shaped((rows, head), B16),
        shaped((rows, wq.shape[1]), B16),
        shaped((rows, 128), F32),
        shaped((rows, 2 * head), F32),
    ]
    out = pl.pallas_call(
        functools.partial(forward_kernel, min(rows, 256)),
        grid_spec=pltpu.PrefetchScalarGridSpec(
            num_scalar_prefetch=1,
            grid=(steps,),
            in_specs=[
                whole(rows, 1), whole(1, rows), whole(*table.shape), whole(rows, width),
                whole(1, width), whole(width, head), whole(width, head), whole(1, head),
                whole(1, head), column(width), pl.BlockSpec((block, width), lambda g, z: (g, 0)),
            ],
            out_specs=[whole(own, width)] * parts + [
                whole(rows, width), column(rows), column(rows), whole(rows, head),
                whole(rows, head), whole(rows, head), column(rows), whole(rows, 128),
                whole(rows, 2 * head),
            ],
            scratch_shapes=[pltpu.VMEM((rows, rows), F32), pltpu.VMEM((rows, width), F32)],
        ),
        out_shape=outs,
        compiler_params=params(),
        cost_estimate=cost(26),
    )(
        z, seq.reshape(rows, 1), seq.reshape(1, rows), table, x, gain.reshape(1, width),
        wk, wv, q_gain.reshape(1, head), k_gain.reshape(1, head), wq, wo,
    )
    return out[:parts], out[parts:]


def norm_back(grads, values, gain):
    scale = norm_scale(values)
    unit = values * scale
    gained = grads * gain
    back = scale * (gained - unit * jnp.mean(gained * unit, axis=-1, keepdims=True))
    return back, jnp.sum(grads * unit, axis=0, keepdims=True)


def backward_kernel(
    tile, parts, first_pair, opening, closing, z_ref,
    seq_col, seq_row, q_gain, wq, wo, q_pre, q_low, k_low, v_low, lse, turns, *refs,
):
    if opening:
        came, refs = refs[:parts], refs[parts:]
    else:
        (branch, acc_in, dkey_in, dvalue_in, gains_in), refs = refs[:5], refs[5:]
    if closing:
        (x, gain, wk, wv, k_gain, k_pre), refs = refs[:6], refs[6:]
        cols, refs = refs[:parts], refs[parts:]
        low, row_scale, gains, bias, acc, dkey, dvalue = refs
    else:
        branch, low, acc, dkey, dvalue, gains, bias = refs
    step = pl.program_id(0)
    last = pl.num_programs(0) - 1
    rows = seq_col.shape[0]
    head = k_low.shape[1]
    per_step = wq.shape[1] // head
    cos, sine = turns[:, :head], turns[:, head:]

    @pl.when(step == 0)
    def _():
        query = lax.broadcasted_iota(jnp.int32, (rows, rows), 0)
        key = lax.broadcasted_iota(jnp.int32, (rows, rows), 1)
        same = seq_col[...] == seq_row[...]
        bias[...] = jnp.where(same & (key <= query), 0.0, -1e30)
        if opening:
            size = came[0].shape[0]
            for d, piece in enumerate(came):
                at = pl.ds(pl.multiple_of((z_ref[0] ^ d) * size, size), size)
                branch[at, :] = piece[...]
            acc[...] = jnp.zeros_like(acc)
            dkey[...] = jnp.zeros_like(dkey)
            dvalue[...] = jnp.zeros_like(dvalue)
            gains[...] = jnp.zeros_like(gains)
        else:
            acc[...] = acc_in[...]
            dkey[...] = dkey_in[...]
            dvalue[...] = dvalue_in[...]
            gains[...] = gains_in[...]

    def heads():
        datt = nt_dot(branch[...], wo[...]).astype(B16)
        lane = lax.broadcasted_iota(jnp.int32, (tile, lse.shape[1]), 1)
        for i in range(per_step):
            at = slice(i * head, (i + 1) * head)
            parts_q = []
            for t in range(rows // tile):
                band = slice(t * tile, (t + 1) * tile)
                seen = (t + 1) * tile
                mine = lane == (first_pair + step) * per_step + i
                logsum = jnp.sum(jnp.where(mine, lse[band, :], 0.0), axis=1, keepdims=True)
                scores = (
                    nt_dot(q_low[band, at], k_low[:seen, :]) * head ** (-0.5) + bias[band, :seen]
                )
                p = jnp.exp(scores - logsum)
                dout = datt[band, at]
                dp = nt_dot(dout, v_low[:seen, :])
                delta = jnp.sum(p * dp, axis=1, keepdims=True)
                ds = (p * (dp - delta)).astype(B16)
                parts_q.append(nn_dot(ds, k_low[:seen, :]) * head ** (-0.5))
                dkey[:seen, :] += tn_dot(ds, q_low[band, at]) * head ** (-0.5)
                dvalue[:seen, :] += tn_dot(p.astype(B16), dout)
            dq = turned_back(jnp.concatenate(parts_q, axis=0), cos, sine)
            back, gain_part = norm_back(dq, q_pre[:, at], q_gain[...])
            low[:, at] = back.astype(B16)
            gains[1:2, :head] += gain_part
        acc[...] += nt_dot(low[...], wq[...])

    if not closing:
        heads()
        return
    pl.when(step < last)(heads)

    @pl.when(step == last)
    def _():
        dk = turned_back(dkey[...], cos, sine)
        back, gain_part = norm_back(dk, k_pre[...], k_gain[...])
        gains[2:3, :head] = gain_part
        low[:, :head] = back.astype(B16)
        low[:, head : 2 * head] = dvalue[...].astype(B16)
        acc[...] += nt_dot(low[:, :head], wk[...]) + nt_dot(low[:, head : 2 * head], wv[...])
        values = x[...].astype(F32)
        total = acc[...]
        along = jnp.sum(total * gain[...] * values, axis=1, keepdims=True)
        gains[3:4, :rows] = jnp.broadcast_to(along, (rows, 128)).T[:1]
        scale = norm_scale(values)
        row_scale[...] = scale
        gains[0:1, :] = jnp.sum(total * (values * scale), axis=0, keepdims=True)
        size = cols[0].shape[1]
        for d, piece in enumerate(cols):
            at = pl.ds(pl.multiple_of((z_ref[0] ^ d) * size, size), size)
            piece[:rows, :] = acc[:, at].astype(B16)
            piece[rows:, :] = jnp.concatenate(
                [gains[3:4, :rows].reshape(1, rows)]
                + [gains[0:1, i * size : (i + 1) * size] for i in range(parts)]
                + [gains[1:2, :size], gains[2:3, :size]]
                + [jnp.zeros((16 - 3 - parts, size), F32)],
                axis=0,
            ).astype(B16)


def attention_backward(z, seq, x, gain, wq, wk, wv, q_gain, k_gain, wo, kept, came, held):
    opening, closing = held is None, held is not None
    rows, width = x.shape
    head = wk.shape[1]
    block = 2 * head
    pairs = wq.shape[1] // block
    half = pairs // 2
    first, steps = (0, half) if opening else (half, pairs - half)
    parts = width // (wo.shape[1] // lax.axis_size("tensor"))
    q_pre, q_low, k_pre, k_low, v_low, lse, turns = kept
    whole = lambda *shape: pl.BlockSpec(shape, lambda g, z: (0,) * len(shape))
    pair_at = lambda g: first + jnp.minimum(g, steps - 1)
    column = lambda height: pl.BlockSpec((height, block), lambda g, z: (0, pair_at(g)))
    state = [whole(rows, width), whole(rows, head), whole(rows, head), whole(8, width)]
    state_shapes = [
        shaped((rows, width), F32), shaped((rows, head), F32), shaped((rows, head), F32),
        shaped((8, width), F32),
    ]
    ins = [
        seq.reshape(rows, 1), seq.reshape(1, rows), q_gain.reshape(1, head), wq, wo,
        q_pre, q_low, k_low, v_low, lse, turns,
    ]
    in_specs = [
        whole(rows, 1), whole(1, rows), whole(1, head), column(width),
        pl.BlockSpec((block, width), lambda g, z: (pair_at(g), 0)),
        column(rows), column(rows), whole(rows, head), whole(rows, head), whole(rows, 128),
        whole(rows, 2 * head),
    ]
    low_block = pl.BlockSpec((rows, block), lambda g, z: (0, g))
    if opening:
        ins = ins + list(came)
        in_specs = in_specs + [whole(rows // parts, width)] * parts
        outs = [shaped((rows, width), B16), shaped((rows, block * steps), B16)] + state_shapes
        out_specs = [whole(rows, width), low_block] + state
        scratch = [pltpu.VMEM((rows, rows), F32)]
    else:
        ins = ins + list(held) + [
            x, gain.reshape(1, width), wk, wv, k_gain.reshape(1, head), k_pre,
        ]
        in_specs = in_specs + [whole(rows, width)] + state + [
            whole(rows, width), whole(1, width), whole(width, head), whole(width, head),
            whole(1, head), whole(rows, head),
        ]
        outs = [shaped((rows + 16, width // parts), B16)] * parts + [
            shaped((rows, block * (steps + 1)), B16), shaped((rows, 1), F32),
        ]
        out_specs = [whole(rows + 16, width // parts)] * parts + [low_block, whole(rows, 1)]
        scratch = [
            pltpu.VMEM((8, width), F32),
            pltpu.VMEM((rows, rows), F32), pltpu.VMEM((rows, width), F32),
            pltpu.VMEM((rows, head), F32), pltpu.VMEM((rows, head), F32),
        ]
    return pl.pallas_call(
        functools.partial(
            backward_kernel, min(rows, 256), parts, first, opening, closing
        ),
        grid_spec=pltpu.PrefetchScalarGridSpec(
            num_scalar_prefetch=1,
            grid=(steps + closing,),
            in_specs=in_specs,
            out_specs=out_specs,
            scratch_shapes=scratch,
        ),
        out_shape=outs,
        compiler_params=params(),
        cost_estimate=cost(16),
    )(z, *ins)


def grads_in_blocks(order, left, rights):
    count = order.shape[0]
    half, high = count // 2, left.shape[1] // count
    wide = sum(v.shape[1] for v in rights)

    def kernel(order_ref, left_ref, *refs):
        right_refs, (send, keep, *whole) = refs[: len(rights)], refs[len(rights) :]
        start = 0
        for ref in right_refs if whole else ():
            end = start + ref.shape[1]
            whole[0][:, start:end] = tn_dot(left_ref[...], ref[...]).astype(B16)
            start = end
        for i in range(count):
            if whole:
                at = pl.ds(pl.multiple_of(order_ref[i] * high, high), high)
                (send, keep)[i // half][i % half] = whole[0][at, :]
                continue
            at = pl.ds(pl.multiple_of(order_ref[i] * high, high), high)
            block = left_ref[:, at]
            out, start = (send, keep)[i // half], 0
            for ref in right_refs:
                end = start + ref.shape[1]
                out[i % half, :, start:end] = tn_dot(block, ref[...]).astype(B16)
                start = end

    return pl.pallas_call(
        kernel,
        in_specs=[SMEM_SPEC] + vmem(1 + len(rights)),
        out_specs=vmem(2),
        out_shape=[shaped((half, high, wide), B16)] * 2,
        scratch_shapes=[pltpu.VMEM((left.shape[1], wide), B16)] if high % 128 else [],
        compiler_params=params(),
        cost_estimate=cost(6),
    )(order, left, *rights)


def halves_after(keep, came):
    half = keep.shape[0] // 2
    return add_low(keep[:half], came[:half]), add_low(keep[half:], came[half:])


def router_kernel(terms, experts, *refs):
    parts, (x, routes, gain, router, middle, packed, shares) = refs[:terms], refs[terms:]
    total = x[...].astype(F32)
    branch = parts[0][...].astype(F32)
    for part in parts[1:]:
        branch = branch + part[...].astype(F32)
    total = total + branch
    middle[...] = total
    width = total.shape[1]
    hidden = (total * norm_scale(total) * gain[...]).astype(B16)
    packed[:, :width] = hidden
    logits = nt_dot(hidden, router[...])
    lane = lax.broadcasted_iota(jnp.int32, logits.shape, 1)
    twin = jnp.where(lane < experts, lane, lane - experts)
    chosen = jnp.zeros(logits.shape, jnp.bool_)
    for k in range(routes.shape[1]):
        chosen = chosen | (twin == routes[:, k : k + 1])
    chosen = chosen & (lane < 2 * experts)
    peak = jnp.max(jnp.where(chosen, logits, -1e30), axis=1, keepdims=True)
    raised = jnp.where(chosen, jnp.exp(jnp.minimum(logits - peak, 0.0)), 0.0)
    share = raised / jnp.sum(jnp.where(lane < experts, raised, 0.0), axis=1, keepdims=True)
    shares[...] = share
    high = share.astype(B16).astype(F32)
    packed[:, width:] = jnp.where(lane < experts, high, share - high).astype(B16)


def row_block(height, width):
    return pl.BlockSpec((height, width), lambda g, z: (z[0], 0))


def route_rows(z, terms, x, routes, gain, router, experts):
    own, width = terms[0].shape
    extra = router.shape[0]
    whole = lambda *shape: pl.BlockSpec(shape, lambda g, z: (0,) * len(shape))
    count = len(terms)

    def kernel(z_ref, *refs):
        router_kernel(count, experts, *refs)

    return pl.pallas_call(
        kernel,
        grid_spec=pltpu.PrefetchScalarGridSpec(
            num_scalar_prefetch=1,
            grid=(1,),
            in_specs=[whole(own, width)] * count + [
                row_block(own, width), row_block(own, routes.shape[1]), whole(1, width),
                whole(extra, width),
            ],
            out_specs=[whole(own, width), whole(own, width + extra), whole(own, extra)],
        ),
        out_shape=[
            shaped((own, width), F32), shaped((own, width + extra), B16), shaped((own, extra), F32),
        ],
        compiler_params=params(),
        cost_estimate=cost(3),
    )(z, *terms, x, routes, gain.reshape(1, width), router)


def rows_back_kernel(count, experts, *refs):
    terms, (dy, middle, shares, gain, router, dbranch, sums) = refs[:count], refs[count:]
    width = middle.shape[1]
    total = terms[0][...].astype(F32)
    for term in terms[1:]:
        total = total + term[...].astype(F32)
    values = middle[...]
    share = shares[...]
    lane = lax.broadcasted_iota(jnp.int32, share.shape, 1)
    dshare = total[:, width:]
    share = jnp.where(lane < experts, share, 0.0)
    mean = jnp.sum(share * dshare, axis=1, keepdims=True)
    dlogits = (share * (dshare - mean)).astype(B16)
    scale = norm_scale(values)
    unit = values * scale
    hidden = (unit * gain[...]).astype(B16)
    dhidden = total[:, :width] + nn_dot(dlogits, router[...])
    gained = dhidden * gain[...]
    back = scale * (gained - unit * jnp.mean(gained * unit, axis=-1, keepdims=True))
    dbranch[...] = (back + dy[...].astype(F32)).astype(B16)
    grads = tn_dot(dlogits, hidden)
    sums[:experts, :] = grads[:experts, :]
    sums[experts:, :] = jnp.broadcast_to(
        jnp.sum(dhidden * unit, axis=0, keepdims=True), (8, width)
    )


def rows_back(z, terms, dy, middle, shares, gain, router, experts):
    own, width = middle.shape
    extra = router.shape[0]
    whole = lambda *shape: pl.BlockSpec(shape, lambda g, z: (0,) * len(shape))
    count = len(terms)

    def kernel(z_ref, *refs):
        rows_back_kernel(count, experts, *refs)

    return pl.pallas_call(
        kernel,
        grid_spec=pltpu.PrefetchScalarGridSpec(
            num_scalar_prefetch=1,
            grid=(1,),
            in_specs=[whole(own, width + extra)] * count + [
                row_block(own, width), whole(own, width), whole(own, extra), whole(1, width),
                whole(extra, width),
            ],
            out_specs=[whole(own, width), whole(experts + 8, width)],
        ),
        out_shape=[shaped((own, width), B16), shaped((experts + 8, width), F32)],
        compiler_params=params(),
        cost_estimate=cost(4),
    )(z, *terms, dy, middle, shares, gain.reshape(1, width), router)


def input_grad_of(z, terms, x, branch, gain, row_scale):
    rows, width = x.shape
    size = terms[0].shape[1]
    below = terms[0].shape[0] - rows
    count = len(terms)

    def kernel(z_ref, *refs):
        parts, (x_ref, branch_ref, gain_ref, scale_ref, out, small) = refs[:count], refs[count:]
        total = parts[0][...].astype(F32)
        for part in parts[1:]:
            total = total + part[...].astype(F32)
        small[...] = total[rows:, :]
        along = jnp.broadcast_to(total[rows : rows + 1, :rows], (128, rows)).T[:, :1]
        scale = scale_ref[...]
        out[...] = branch_ref[...].astype(F32) + scale * (
            total[:rows, :] * gain_ref[...]
            - x_ref[...].astype(F32) * (scale * scale * (along * (1.0 / width)))
        )

    whole = lambda *shape: pl.BlockSpec(shape, lambda g, z: (0,) * len(shape))
    column = lambda height: pl.BlockSpec((height, size), lambda g, z: (0, z[0]))
    return pl.pallas_call(
        kernel,
        grid_spec=pltpu.PrefetchScalarGridSpec(
            num_scalar_prefetch=1,
            grid=(1,),
            in_specs=[whole(rows + below, size)] * count + [
                column(rows), column(rows), column(1), whole(rows, 1),
            ],
            out_specs=[whole(rows, size), whole(below, size)],
        ),
        out_shape=[shaped((rows, size), F32), shaped((below, size), F32)],
        compiler_params=params(),
        cost_estimate=cost(3),
    )(z, *terms, x, branch, gain.reshape(1, width), row_scale)


def expert_kernel(places, group, slots, hidden, experts, *refs):
    parts = len(places)
    z_ref, ids_ref, refs = refs[0], refs[1], refs[2:]
    packed, refs = refs[:parts], refs[parts:]
    dy, refs = refs[0], refs[1:]
    weights, refs = refs[: 3 * group], refs[3 * group :]
    backs, refs = refs[:parts], refs[parts:]
    held, dgu_out, act_out, gate_up, down, dgu_buf, act_buf, total, sems, out_sems = refs
    rows, width = dy.shape
    pair = 2 * hidden
    size = rows // parts
    extra = held.shape[1] - width

    def fetch(d):
        slot = d % slots
        gate, up, dn = weights[3 * d : 3 * d + 3]
        return [
            pltpu.make_async_copy(gate, gate_up.at[slot, :pair], sems.at[0, slot]),
            pltpu.make_async_copy(up, gate_up.at[slot, pair:], sems.at[1, slot]),
            pltpu.make_async_copy(dn, down.at[slot], sems.at[2, slot]),
        ]

    def store(d):
        return [
            pltpu.make_async_copy(dgu_buf.at[d % 2], dgu_out.at[d], out_sems.at[0, d % 2]),
            pltpu.make_async_copy(act_buf.at[d % 2], act_out.at[d], out_sems.at[1, d % 2]),
        ]

    for copy in fetch(0):
        copy.start()
    for d in range(1, min(slots, group)):
        for copy in fetch(d):
            copy.start()

    def rows_of(d):
        return pl.ds(pl.multiple_of((z_ref[0] ^ d) * size, size), size)

    for i, d in enumerate(places):
        held[rows_of(d), :] = packed[i][...]
    shares = held[:, width:].astype(F32)
    lane = lax.broadcasted_iota(jnp.int32, (rows, extra), 1)
    first = lax.broadcasted_iota(jnp.int32, (rows, pair), 1) < hidden

    def share_of(expert):
        mine = (lane == expert) | (lane == expert + experts)
        return jnp.sum(jnp.where(mine, shares, 0.0), axis=1, keepdims=True)

    dshares = jnp.zeros((rows, extra), F32)
    for d in range(group):
        slot = d % slots
        for copy in fetch(d):
            copy.wait()
        id_a, id_b = ids_ref[2 * d], ids_ref[2 * d + 1]
        both = nt_dot(held[:, :width], gate_up[slot])
        raw = nt_dot(dy[...], down[slot])
        gate, up = both[:, :pair], both[:, pair:]
        share = jnp.where(first, share_of(id_a), share_of(id_b))
        sig = 1.0 / (1.0 + jnp.exp(-gate))
        silu = gate * sig
        act = (silu * up).astype(B16).astype(F32)
        product = act * raw
        part_a = jnp.sum(jnp.where(first, product, 0.0), axis=1, keepdims=True)
        part_b = jnp.sum(jnp.where(first, 0.0, product), axis=1, keepdims=True)
        dshares = dshares + jnp.where(lane == id_a, part_a, 0.0)
        dshares = dshares + jnp.where(lane == id_b, part_b, 0.0)
        dact = share * raw
        dgate = dact * up * (sig * (1.0 + gate * (1.0 - sig)))
        dup = dact * silu
        if d >= 2:
            for copy in store(d - 2):
                copy.wait()
        dgu_buf[d % 2, :, :pair] = dgate.astype(B16)
        dgu_buf[d % 2, :, pair:] = dup.astype(B16)
        act_buf[d % 2] = (share * act).astype(B16)
        for copy in store(d):
            copy.start()
        term = nn_dot(dgu_buf[d % 2], gate_up[slot])
        total[...] = term if d == 0 else total[...] + term
        if d + slots < group:
            for copy in fetch(d + slots):
                copy.start()
    for i, d in enumerate(places):
        backs[i][:, :width] = total[rows_of(d), :].astype(B16)
    total[:, :extra] = dshares
    for i, d in enumerate(places):
        backs[i][:, width:] = total[rows_of(d), :extra].astype(B16)
    for d in range(max(0, group - 2), group):
        for copy in store(d):
            copy.wait()


def expert_pass(z, ids, places, packed, dy, weights, experts):
    width = dy.shape[1]
    parts = len(places)
    size, full = packed[0].shape
    rows = size * parts
    group = len(weights)
    pair = weights[0][0].shape[0]
    slots = min(group, 4)
    out = pl.pallas_call(
        functools.partial(expert_kernel, tuple(places), group, slots, pair // 2, experts),
        in_specs=[SMEM_SPEC, SMEM_SPEC] + vmem(parts + 1) + hbm(3 * group),
        out_specs=vmem(parts + 1) + hbm(2),
        out_shape=[shaped((size, full), B16)] * parts + [
            shaped((rows, full), B16),
            shaped((group, rows, 2 * pair), B16),
            shaped((group, rows, pair), B16),
        ],
        scratch_shapes=[
            pltpu.VMEM((slots, 2 * pair, width), B16),
            pltpu.VMEM((slots, pair, width), B16),
            pltpu.VMEM((2, rows, 2 * pair), B16),
            pltpu.VMEM((2, rows, pair), B16),
            pltpu.VMEM((rows, width), F32),
            pltpu.SemaphoreType.DMA((3, slots)),
            pltpu.SemaphoreType.DMA((2, 2)),
        ],
        compiler_params=params(58),
        cost_estimate=cost(31),
    )(z, ids, *packed, dy, *[w for three in weights for w in three])
    return dict(zip(places, out[:parts])), out[parts:]


def outputs_kernel(parts, sources, group, z_ref, middle, *refs):
    acts, refs = refs[:sources], refs[sources:]
    downs, outs, total = refs[:group], refs[group:-1], refs[-1]
    size = outs[0].shape[1]
    for s in range(sources):
        value = nn_dot(acts[s][0], downs[0][...])
        for d in range(1, group):
            value = value + nn_dot(acts[s][d], downs[d][...])
        total[...] = value
        if s == 0:
            own = middle.shape[0]
            total[pl.ds(pl.multiple_of(z_ref[0] * own, own), own), :] += middle[...]
        for d in range(parts):
            at = pl.ds(pl.multiple_of((z_ref[0] ^ d) * size, size), size)
            outs[s * parts + d][...] = total[:, at].astype(B16)


def expert_outputs(z, middle, acts, downs, parts):
    group, rows, pair = acts[0].shape
    width = downs[0].shape[1]
    count = len(acts) * parts
    return pl.pallas_call(
        functools.partial(outputs_kernel, parts, len(acts), group),
        in_specs=[SMEM_SPEC] + vmem(1 + len(acts) + group),
        out_specs=vmem(count),
        out_shape=[shaped((rows, width // parts), B16)] * count,
        scratch_shapes=[pltpu.VMEM((rows, width), F32)],
        compiler_params=params(),
        cost_estimate=cost(10),
    )(z, middle, *acts, *downs)


def grads_kernel(sources, *refs):
    ins, out = refs[:-1], refs[-1]
    width = out.shape[1]

    def write(part):
        total = 0.0
        for s in range(sources):
            held, dy, dgu, act = ins[4 * s : 4 * s + 4]
            if part < 2:
                total = total + tn_dot(dgu[0], held[:, :width])
            else:
                total = total + tn_dot(act[0], dy[...])
        out[...] = total.astype(B16)

    step = pl.program_id(0)
    pl.when(step < 2)(functools.partial(write, 0))
    pl.when(step == 2)(functools.partial(write, 2))


def expert_grads(distance, sources):
    pair, width = sources[0][3].shape[2], sources[0][1].shape[1]
    whole = lambda *shape: pl.BlockSpec(shape, lambda g: (0,) * len(shape))
    return pl.pallas_call(
        functools.partial(grads_kernel, len(sources)),
        grid=(3,),
        in_specs=[
            spec
            for held, dy, dgu, act in sources
            for spec in (
                whole(*held.shape),
                whole(*dy.shape),
                pl.BlockSpec((1, held.shape[0], pair), lambda g: (distance, 0, jnp.minimum(g, 1))),
                pl.BlockSpec((1, held.shape[0], pair), lambda g: (distance, 0, 0)),
            )
        ],
        out_specs=pl.BlockSpec((pair, width), lambda g: (g, 0)),
        out_shape=shaped((3 * pair, width), B16),
        compiler_params=params(),
        cost_estimate=cost(11),
    )(*[v for source in sources for v in source])


def sum_of_grads(wholes, pieces):
    rows, width = wholes[0].shape
    block = min(width, 512)
    size = pieces[0].shape[0]
    count = len(wholes)
    each = rows // 3

    def kernel(*refs):
        parts, refs = refs[:count], refs[count:]
        more, outs = refs[:-3], refs[-3:]
        for i, piece in enumerate(more):
            total = piece[...].astype(F32)
            for part in parts:
                total = total + part[i * size : (i + 1) * size, :].astype(F32)
            at = i * size % each
            outs[i * size // each][at : at + size, :] = total

    line = lambda height: pl.BlockSpec((height, block), lambda g: (0, g))
    return pl.pallas_call(
        kernel,
        grid=(width // block,),
        in_specs=[line(rows)] * count + [line(size)] * len(pieces),
        out_specs=[line(each)] * 3,
        out_shape=[shaped((each, width), F32)] * 3,
        compiler_params=params(),
        cost_estimate=cost(8),
    )(*wholes, *pieces)


def per_device(
    tokens,
    sequence_numbers,
    routes,
    attn_gain,
    w_query,
    key_projection,
    value_projection,
    query_gain,
    key_gain,
    w_out,
    moe_gain,
    w_router,
    w_gate,
    w_up,
    w_down,
    cotangent,
):
    tok_count, model_width = tokens.shape
    head_dim = query_gain.shape[0]
    tensor_size = lax.axis_size("tensor")
    tensor_pos = lax.axis_index("tensor")
    expert_size = lax.axis_size("expert")
    expert_pos = lax.axis_index("expert")
    local_experts, _, hidden = w_gate.shape
    experts = local_experts * expert_size
    pair = local_experts * hidden
    group = 2 << ((expert_size // 2).bit_length() // 2)
    rounds = expert_size // group
    own_rows = tok_count // tensor_size
    everyone = list(range(tensor_size))
    z = tensor_pos.astype(jnp.int32).reshape(1)

    weights = [
        {0: jnp.swapaxes(w_gate, 1, 2).reshape(pair, model_width)},
        {0: jnp.swapaxes(w_up, 1, 2).reshape(pair, model_width)},
        {0: w_down.reshape(pair, model_width)},
    ]
    for held in weights:
        for bit in reversed(range(1, group.bit_length() - 1)):
            held.update({d ^ (1 << bit): swap(v, "expert", 1 << bit) for d, v in list(held.items())})
    ids = jnp.concatenate(
        [(expert_pos ^ d) * local_experts + jnp.arange(local_experts) for d in range(group)]
    ).astype(jnp.int32)
    dy_own = lax.all_gather(cotangent, "tensor", axis=1, tiled=True)

    attention = (
        z, sequence_numbers, tokens, attn_gain, w_query, key_projection, value_projection,
        query_gain, key_gain, w_out,
    )
    branch_parts, kept = attention_forward(*attention, tensor_size)
    first_hidden, attended_low = kept[0], kept[6]
    kept = kept[1:6] + kept[7:]
    branch_came = exchange_near(branch_parts, "tensor")
    for d in everyone[2::2]:
        branch_came[d], weights[0] = together(branch_came[d], weights[0])
    dy_own = after(dy_own, branch_came[2])
    dy_of = [dy_own] + [swap(dy_own, "expert", group * r) for r in range(1, rounds)]
    terms = [branch_parts[0], branch_came[0]] + further_terms(branch_parts, branch_came, "tensor")
    terms, weights[1] = together(terms, weights[1])

    router_rows = jnp.swapaxes(w_router, 0, 1)
    spare = -(2 * experts) % 128
    router_rows = jnp.concatenate(
        [router_rows, router_rows, jnp.zeros((spare, model_width), B16)], axis=0
    )
    middle, packed_rows, shares = route_rows(
        z, terms, tokens, routes, moe_gain, router_rows, experts
    )
    for i in range(2):
        weights[i] = after(weights[i], packed_rows)
        weights[i].update({d ^ 1: swap(v, "expert", 1) for d, v in list(weights[i].items())})
    packed_of = [{0: packed_rows}] + [
        {0: swap(packed_rows, "expert", group * r)} for r in range(1, rounds)
    ]
    top = bits_of("tensor") - 1
    first = {1 << bit: swap(packed_rows, "tensor", 1 << bit) for bit in range(top + 1)}
    first, weights[2] = together(first, weights[2])
    weights[2].update({d ^ 1: swap(v, "expert", 1) for d, v in list(weights[2].items())})
    packed_of[0].update(first)
    for bit in reversed(range(top)):
        came = {
            d | 1 << bit: swap(v, "tensor", 1 << bit)
            for d, v in packed_of[0].items() if d and not d & ((2 << bit) - 1)
        }
        packed_of[0].update(after(came, [p[0] for p in packed_of[1:]], dy_of[1:]))
    for r in range(1, rounds):
        packed_of[r].update(
            {d: swap(v, "expert", group * r) for d, v in packed_of[0].items() if d}
        )
    weights = [[held[d] for held in weights] for d in range(group)]

    far = [d for d in everyone if d & 1][::-1]
    near = [d for d in everyone if not d & 1][::-1]
    back, sources = [], []
    for r in range(rounds):
        part, extra = expert_pass(
            after(z, [b[0] for b in back]), ids, everyone,
            [packed_of[r][d] for d in everyone], dy_of[r], weights, experts,
        )
        if r:
            part = {d: swap(part[d], "expert", group * r) for d in far + near}
        back.append(part)
        sources.append((extra[0], dy_of[r], extra[1], extra[2]))

    downs = [w[2] for w in weights]
    joined = [None] * tensor_size
    made, odd, high, passed = {}, {}, {}, {}
    mask = group // 2
    outs = expert_outputs(
        z, middle, [source[3] for source in sources], downs, tensor_size
    )
    for place in far:
        joined[place] = add_low(*after([b[place] for b in back], outs[0]))
    last = [joined[place] for place in far]
    for d in range(group - 1, mask - 1, -1):
        made[d] = expert_grads(d, after(sources, last))
        last = [made[d]]
        if d == group - 1:
            for place in near[:-1]:
                joined[place] = add_low(*after([b[place] for b in back], last))
                last = last + [joined[place]]
    for d in range(group - 1, mask - 1, -2):
        odd[d - 1] = swap(after(made[d], last), "expert", 1)
    for d in range(group - 2, mask - 1, -2):
        mine_all, theirs_all = after([made[d], odd[d]], last)
        high[d] = [
            add_low(mine_all[i * hidden : (i + 1) * hidden], theirs_all[i * hidden : (i + 1) * hidden])
            for i in range(3 * local_experts)
        ]
        passed[d - mask] = [swap(v, "expert", mask) for v in high[d]]
    out_own = outs[:tensor_size]
    out_came = [
        {d: swap(outs[r * tensor_size + d], "expert", group * r) for d in far + near}
        for r in range(1, rounds)
    ]

    def pieces_at(*places):
        return [v[i] for v in passed.values() for i in places]

    back_terms = [b[0] for b in back] + scatter_terms_of(joined, "tensor")
    shape = (local_experts, hidden, model_width)

    back_terms = after(
        back_terms, last, [came[far[0]] for came in out_came]
    )
    dbranch, row_sums = rows_back(
        z, back_terms, dy_own, middle, shares, moe_gain, router_rows, experts
    )
    def share_step(small, bit):
        small = small.reshape((small.shape[0], -1, 2, model_width // expert_size))
        mine = (expert_pos >> bit) & 1
        send = lax.dynamic_index_in_dim(small, 1 - mine, 2, False)
        keep = lax.dynamic_index_in_dim(small, mine, 2, False)
        return keep, swap(send, "expert", 1 << bit)

    row_share = row_sums[: experts + 1]
    row_keep, row_came = share_step(row_share, 0)
    lower = list(range(group // 2 - 1, -1, -1))
    pieces, last = {0: dbranch}, dbranch
    for bit in reversed(range(bits_of("tensor"))):
        came = {d ^ (1 << bit): swap(v, "tensor", 1 << bit) for d, v in pieces.items()}
        share_lower = -(-len(lower) // bits_of("tensor"))
        place = bits_of("tensor") - 1 - bit
        for d in lower[place * share_lower : (place + 1) * share_lower]:
            made[d] = expert_grads(d, after(sources, last))
            if d & 1:
                odd[d - 1] = swap(made[d], "expert", 1)
            last = made[d]
        came = after(came, last)
        if bit:
            came = after(came, [came_r[far[-1]] for came_r in out_came], pieces_at(0))
        else:
            came = after(came, pieces_at(1), [came_r[d] for came_r in out_came for d in near if d])
        pieces.update(came)
        last = came
    dbranch_pieces = [pieces[d] for d in everyone]
    mine = {d: [made[d], odd[d]] for d in range(0, mask, 2)}
    theirs = passed
    while mask > 2:
        sums = {d: add_low(*v, jnp.concatenate(theirs[d], axis=0)) for d, v in mine.items()}
        mask //= 2
        theirs = {
            d - mask: [
                swap(sums[d][i * hidden : (i + 1) * hidden], "expert", mask)
                for i in range(3 * local_experts)
            ]
            for d in sums if d >= mask
        }
        mine = {d: [sums[d]] for d in sums if d < mask}
    out_parts = [None] * tensor_size
    for d in far:
        came = after([came_r[d] for came_r in out_came], dbranch_pieces)
        out_parts[d] = add_low(out_own[d], *came)
    out_far = exchange_near(out_parts, "tensor")

    branch_low = jnp.zeros((tok_count, model_width), B16)
    for d, v in enumerate(dbranch_pieces):
        at = (tensor_pos ^ d) * v.shape[0]
        branch_low = lax.dynamic_update_slice_in_dim(branch_low, v, at, 0)
    order = expert_pos ^ jnp.asarray(
        list(range(1, expert_size, 2)) + list(range(0, expert_size, 2)), jnp.int32
    )
    far_bits = list(reversed(range(1, bits_of("expert"))))
    wo_send, wo_keep = grads_in_blocks(order, branch_low, [attended_low])
    wo_came = swap(wo_send, "expert", 1)
    dbranch_pieces = after(dbranch_pieces, wo_keep)
    branch_low, low_first, *held = attention_backward(*attention, kept, dbranch_pieces, None)
    wo_keep, wo_send = halves_after(wo_keep, wo_came)
    held, out_came, out_far, theirs[0][2], wo_send, wo_keep = together(
        held, out_came, out_far, theirs[0][2], wo_send, wo_keep
    )
    wo_came = swap(wo_send, "expert", 1 << far_bits[0])
    for d in near:
        if d:
            out_parts[d] = add_low(out_own[d], *[came_r[d] for came_r in out_came])
    out_terms = [out_own[0]] + [came_r[0] for came_r in out_came]
    out_came = out_far
    out_sums = {d: add_low(out_parts[d], v) if d else None for d, v in out_came.items()}
    row_keep, row_came = share_step(row_keep + row_came, 1)
    held = after(held, out_sums)
    out_terms = out_terms + [out_came[0]] + passed_on(out_sums, "tensor")
    *cols_out, low_last, row_scale = attention_backward(
        *attention, kept, None, [branch_low] + held
    )
    col_parts = cols_out
    for bit in range(2, bits_of("expert")):
        row_keep, row_came = share_step(row_keep + row_came, bit)
    low_last, theirs[0][3], wo_came, out_terms = together(
        low_last, theirs[0][3], wo_came, out_terms
    )
    row_share = (row_keep + row_came).reshape(experts + 1, -1)
    for bit in far_bits[1:]:
        wo_keep, wo_send = halves_after(wo_keep, wo_came)
        wo_came = swap(wo_send, "expert", 1 << bit)
    col_came = exchange_near(col_parts, "tensor")
    q_send, q_keep = grads_in_blocks(order, first_hidden, [low_first, low_last])
    q_came = swap(q_send, "expert", 1)
    q_keep, q_send = halves_after(q_keep, q_came)
    q_came = swap(q_send, "expert", 1 << far_bits[0])
    col_came = after(col_came, theirs[0][4], q_send)
    gate_flat, up_flat, down_flat = sum_of_grads(mine[0], theirs[0])
    gate_grad = jnp.swapaxes(gate_flat.reshape(shape), 1, 2)
    up_grad = jnp.swapaxes(up_flat.reshape(shape), 1, 2)
    down_grad = down_flat.reshape(shape)
    col_terms = [col_parts[0], col_came[0]] + further_terms(col_parts, col_came, "tensor")
    for bit in far_bits[1:]:
        q_keep, q_send = halves_after(q_keep, q_came)
        q_came = swap(q_send, "expert", 1 << bit)
    out_weight_grad = (wo_keep[0].astype(F32) + wo_came[0].astype(F32)).T
    col_terms = after(col_terms, q_came, wo_came, gate_flat, row_share)
    input_grad, small = input_grad_of(z, col_terms, tokens, branch_low, attn_gain, row_scale)
    gains = small[1 : 1 + tensor_size].reshape(1, model_width)
    qkv = q_keep[0].astype(F32) + q_came[0].astype(F32)
    q_size = w_query.shape[1]

    def share_of_sum(small):
        small = small.reshape((small.shape[0],) + (2,) * bits_of("expert") + (-1,))
        for bit in range(bits_of("expert")):
            dim = small.ndim - 2
            mine = (expert_pos >> bit) & 1
            send = lax.dynamic_index_in_dim(small, 1 - mine, dim, False)
            keep = lax.dynamic_index_in_dim(small, mine, dim, False)
            small = keep + swap(send, "expert", 1 << bit)
        return small

    columns_each = model_width // expert_size
    head_each = head_dim // expert_size
    spread = jnp.pad(
        small[1 + tensor_size : 3 + tensor_size, :head_dim].reshape(2, expert_size, head_each),
        ((0, 0), (0, 0), (0, columns_each - head_each)),
    )
    small = share_of_sum(jnp.concatenate([gains, spread.reshape(2, model_width)], axis=0))
    row_share = sum_everywhere(after(row_share, input_grad), "tensor")
    mixed = functools.reduce(jnp.add, [t.astype(F32) for t in out_terms])
    block_out = mixed.astype(B16)

    return (
        block_out,
        input_grad,
        small[0],
        qkv[:, :q_size],
        qkv[:, q_size : q_size + head_dim],
        qkv[:, q_size + head_dim :],
        small[1, :head_each],
        small[2, :head_each],
        out_weight_grad,
        row_share[experts],
        jnp.swapaxes(row_share[:experts], 0, 1),
        gate_grad,
        up_grad,
        down_grad,
    )


def solution(mesh):
    placed = (
        P("expert", None),
        P("expert"),
        P("expert", None),
        P(),
        P(None, "tensor"),
        P(None, "tensor"),
        P(None, "tensor"),
        P(),
        P(),
        P("tensor", None),
        P(),
        P(),
        P("expert", None, "tensor"),
        P("expert", None, "tensor"),
        P("expert", "tensor", None),
        P("expert", "tensor"),
    )
    return jax.shard_map(
        per_device,
        mesh=mesh,
        in_specs=placed,
        out_specs=(
            P("expert", "tensor"),
            P("expert", "tensor"),
            P("expert"),
            P("expert", "tensor"),
            P("expert", "tensor"),
            P("expert", "tensor"),
            P("expert"),
            P("expert"),
            P("tensor", "expert"),
            P("expert"),
            P("expert", None),
            P("expert", None, "tensor"),
            P("expert", None, "tensor"),
            P("expert", "tensor", None),
        ),
        check_vma=False,
    )
```

```python
import functools

import jax
import jax.numpy as jnp
import ml_dtypes
import numpy as np
from jax import lax
from jax.experimental import pallas as pl
from jax.experimental.pallas import tpu as pltpu
from jax.sharding import PartitionSpec as P

F32 = jnp.float32
B16 = jnp.bfloat16
EPS = 1e-06


def swap(values, axis, mask):
    count = lax.axis_size(axis)
    return lax.ppermute(values, axis, [(i, i ^ mask) for i in range(count)])


def bits_of(axis):
    return lax.axis_size(axis).bit_length() - 1


def scatter_terms_of(pieces, axis):
    held = {d: v for d, v in enumerate(pieces)}
    terms = []
    for bit in range(bits_of(axis)):
        mask = 1 << bit
        came = {d: swap(held[d ^ mask], axis, mask) for d in held if not d & mask}
        terms.append(came[0])
        held = {d: add_low(held[d], v) if d else None for d, v in came.items()}
    return terms


def after(values, *others):
    return lax.optimization_barrier((values, others))[0]


def further_terms(pieces, came, axis):
    return passed_on({d: add_low(pieces[d], v) if d else None for d, v in came.items()}, axis)


def passed_on(held, axis):
    terms = []
    for bit in range(1, bits_of(axis)):
        mask = 1 << bit
        came = {d: swap(held[d ^ mask], axis, mask) for d in held if not d & mask}
        terms.append(came[0])
        held = {d: add_low(held[d], v) if d else None for d, v in came.items()}
    return terms


def exchange_near(pieces, axis):
    return {d: swap(pieces[d ^ 1], axis, 1) for d in range(lax.axis_size(axis) - 2, -1, -2)}


def together(*values):
    return lax.optimization_barrier(values)


def add_low(*values):
    return functools.reduce(jnp.add, [v.astype(F32) for v in values]).astype(B16)


def sum_everywhere(values, axis):
    for bit in range(bits_of(axis)):
        values = values + swap(values, axis, 1 << bit)
    return values


def nn_dot(left, right):
    return jnp.dot(left, right, preferred_element_type=F32)


def nt_dot(left, right):
    return lax.dot_general(left, right, (((1,), (1,)), ((), ())), preferred_element_type=F32)


def tn_dot(left, right):
    return lax.dot_general(left, right, (((0,), (0,)), ((), ())), preferred_element_type=F32)


def vmem(*count):
    return [pl.BlockSpec(memory_space=pltpu.VMEM) for _ in range(count[0])]


def hbm(count):
    return [pl.BlockSpec(memory_space=pl.ANY) for _ in range(count)]


SMEM_SPEC = pl.BlockSpec(memory_space=pltpu.SMEM)


def params(mib=56):
    return pltpu.CompilerParams(vmem_limit_bytes=mib << 20)


PACE = 3.0


def cost(micros):
    moved = int(micros * PACE * 3.6e6)
    return pl.CostEstimate(flops=0, bytes_accessed=moved, transcendentals=0)


def shaped(shape, dtype):
    return jax.ShapeDtypeStruct(shape, dtype)


def rope_table(length, head_dim):
    half = head_dim // 2
    frequency = np.power(1000000.0, -2.0 * np.arange(half, dtype=np.float32) / head_dim)
    angles = np.arange(length, dtype=np.float32)[:, None] * frequency.astype(np.float32)[None, :]
    angles = angles.astype(np.float64)
    rest = np.concatenate(
        [np.cos(angles), np.cos(angles), -np.sin(angles), np.sin(angles)], axis=1
    )
    terms = []
    for _ in range(3):
        term = rest.astype(np.float32).astype(ml_dtypes.bfloat16)
        terms.append(term)
        rest = rest - term.astype(np.float64)
    return np.concatenate(terms, axis=1)


def norm_scale(values):
    return lax.rsqrt(jnp.mean(values * values, axis=-1, keepdims=True) + EPS)


def turned(values, cos, sine):
    return values * cos + pltpu.roll(values, values.shape[-1] // 2, 1) * sine


def turned_back(grads, cos, sine):
    return grads * cos + pltpu.roll(grads * sine, grads.shape[-1] // 2, 1)


def forward_kernel(
    tile, z_ref,
    seq_col, seq_row, table, x, gain, wk, wv, q_gain, k_gain, wq, wo,
    *refs,
):
    pieces, refs = refs[:-11], refs[-11:]
    h1, q_pre, q_low, k_pre, k_low, v_low, att, lse, turns, bias, acc = refs
    step = pl.program_id(0)
    rows = x.shape[0]
    head = wk.shape[1]
    per_step = wq.shape[1] // head

    @pl.when(step == 0)
    def _():
        values = x[...].astype(F32)
        h1[...] = (values * norm_scale(values) * gain[...]).astype(B16)
        query = lax.broadcasted_iota(jnp.int32, (rows, rows), 0)
        key = lax.broadcasted_iota(jnp.int32, (rows, rows), 1)
        same = seq_col[...] == seq_row[...]
        position = jnp.sum(jnp.where(same & (key < query), 1.0, 0.0), axis=1, keepdims=True)
        bias[...] = jnp.where(same & (key <= query), 0.0, -1e30)
        chosen = jnp.where(key == position.astype(jnp.int32), 1.0, 0.0).astype(B16)
        three = nn_dot(chosen, table[...])
        wide = 2 * head
        turns[...] = three[:, :wide] + three[:, wide : 2 * wide] + three[:, 2 * wide :]
        keys = nn_dot(h1[...], wk[...])
        k_pre[...] = keys
        k_low[...] = turned(
            keys * norm_scale(keys) * k_gain[...], turns[:, :head], turns[:, head:]
        ).astype(B16)
        v_low[...] = nn_dot(h1[...], wv[...]).astype(B16)
        lse[...] = jnp.zeros_like(lse)
        acc[...] = jnp.zeros_like(acc)

    queries = nn_dot(h1[...], wq[...])
    q_pre[...] = queries
    lane = lax.broadcasted_iota(jnp.int32, (tile, lse.shape[1]), 1)
    for i in range(per_step):
        at = slice(i * head, (i + 1) * head)
        mine = queries[:, at]
        q_low[:, at] = turned(
            mine * norm_scale(mine) * q_gain[...], turns[:, :head], turns[:, head:]
        ).astype(B16)
        for t in range(rows // tile):
            band = slice(t * tile, (t + 1) * tile)
            seen = (t + 1) * tile
            scores = nt_dot(q_low[band, at], k_low[:seen, :]) * head ** (-0.5) + bias[band, :seen]
            peak = jnp.max(scores, axis=1, keepdims=True)
            shares = jnp.exp(scores - peak)
            total = jnp.sum(shares, axis=1, keepdims=True)
            att[band, at] = nn_dot((shares / total).astype(B16), v_low[:seen, :]).astype(B16)
            lse[band, :] += jnp.where(lane == step * per_step + i, peak + jnp.log(total), 0.0)
    acc[...] += nn_dot(att[...], wo[...])

    @pl.when(step == pl.num_programs(0) - 1)
    def _():
        size = pieces[0].shape[0]
        for d, piece in enumerate(pieces):
            piece[...] = acc[pl.ds(pl.multiple_of((z_ref[0] ^ d) * size, size), size), :].astype(B16)


def attention_forward(z, seq, x, gain, wq, wk, wv, q_gain, k_gain, wo, parts):
    rows, width = x.shape
    head = wk.shape[1]
    block = min(2 * head, wq.shape[1])
    steps = wq.shape[1] // block
    table = jnp.asarray(rope_table(rows, head))
    whole = lambda *shape: pl.BlockSpec(shape, lambda g, z: (0,) * len(shape))
    column = lambda height: pl.BlockSpec((height, block), lambda g, z: (0, g))
    own = rows // parts
    outs = [shaped((own, width), B16)] * parts + [
        shaped((rows, width), B16),
        shaped((rows, wq.shape[1]), F32),
        shaped((rows, wq.shape[1]), B16),
        shaped((rows, head), F32),
        shaped((rows, head), B16),
        shaped((rows, head), B16),
        shaped((rows, wq.shape[1]), B16),
        shaped((rows, 128), F32),
        shaped((rows, 2 * head), F32),
    ]
    out = pl.pallas_call(
        functools.partial(forward_kernel, min(rows, 256)),
        grid_spec=pltpu.PrefetchScalarGridSpec(
            num_scalar_prefetch=1,
            grid=(steps,),
            in_specs=[
                whole(rows, 1), whole(1, rows), whole(*table.shape), whole(rows, width),
                whole(1, width), whole(width, head), whole(width, head), whole(1, head),
                whole(1, head), column(width), pl.BlockSpec((block, width), lambda g, z: (g, 0)),
            ],
            out_specs=[whole(own, width)] * parts + [
                whole(rows, width), column(rows), column(rows), whole(rows, head),
                whole(rows, head), whole(rows, head), column(rows), whole(rows, 128),
                whole(rows, 2 * head),
            ],
            scratch_shapes=[pltpu.VMEM((rows, rows), F32), pltpu.VMEM((rows, width), F32)],
        ),
        out_shape=outs,
        compiler_params=params(),
        cost_estimate=cost(26),
    )(
        z, seq.reshape(rows, 1), seq.reshape(1, rows), table, x, gain.reshape(1, width),
        wk, wv, q_gain.reshape(1, head), k_gain.reshape(1, head), wq, wo,
    )
    return out[:parts], out[parts:]


def norm_back(grads, values, gain):
    scale = norm_scale(values)
    unit = values * scale
    gained = grads * gain
    back = scale * (gained - unit * jnp.mean(gained * unit, axis=-1, keepdims=True))
    return back, jnp.sum(grads * unit, axis=0, keepdims=True)


def backward_kernel(
    tile, parts, first_pair, opening, closing, z_ref,
    seq_col, seq_row, q_gain, wq, wo, q_pre, q_low, k_low, v_low, lse, turns, *refs,
):
    if opening:
        came, refs = refs[:parts], refs[parts:]
    else:
        (branch, acc_in, dkey_in, dvalue_in, gains_in), refs = refs[:5], refs[5:]
    if closing:
        (x, gain, wk, wv, k_gain, k_pre), refs = refs[:6], refs[6:]
        cols, refs = refs[:parts], refs[parts:]
        low, row_scale, gains, bias, acc, dkey, dvalue = refs
    else:
        branch, low, acc, dkey, dvalue, gains, bias = refs
    step = pl.program_id(0)
    last = pl.num_programs(0) - 1
    rows = seq_col.shape[0]
    head = k_low.shape[1]
    per_step = wq.shape[1] // head
    cos, sine = turns[:, :head], turns[:, head:]

    @pl.when(step == 0)
    def _():
        query = lax.broadcasted_iota(jnp.int32, (rows, rows), 0)
        key = lax.broadcasted_iota(jnp.int32, (rows, rows), 1)
        same = seq_col[...] == seq_row[...]
        bias[...] = jnp.where(same & (key <= query), 0.0, -1e30)
        if opening:
            size = came[0].shape[0]
            for d, piece in enumerate(came):
                at = pl.ds(pl.multiple_of((z_ref[0] ^ d) * size, size), size)
                branch[at, :] = piece[...]
            acc[...] = jnp.zeros_like(acc)
            dkey[...] = jnp.zeros_like(dkey)
            dvalue[...] = jnp.zeros_like(dvalue)
            gains[...] = jnp.zeros_like(gains)
        else:
            acc[...] = acc_in[...]
            dkey[...] = dkey_in[...]
            dvalue[...] = dvalue_in[...]
            gains[...] = gains_in[...]

    def heads():
        datt = nt_dot(branch[...], wo[...]).astype(B16)
        lane = lax.broadcasted_iota(jnp.int32, (tile, lse.shape[1]), 1)
        for i in range(per_step):
            at = slice(i * head, (i + 1) * head)
            parts_q = []
            for t in range(rows // tile):
                band = slice(t * tile, (t + 1) * tile)
                seen = (t + 1) * tile
                mine = lane == (first_pair + step) * per_step + i
                logsum = jnp.sum(jnp.where(mine, lse[band, :], 0.0), axis=1, keepdims=True)
                scores = (
                    nt_dot(q_low[band, at], k_low[:seen, :]) * head ** (-0.5) + bias[band, :seen]
                )
                p = jnp.exp(scores - logsum)
                dout = datt[band, at]
                dp = nt_dot(dout, v_low[:seen, :])
                delta = jnp.sum(p * dp, axis=1, keepdims=True)
                ds = (p * (dp - delta)).astype(B16)
                parts_q.append(nn_dot(ds, k_low[:seen, :]) * head ** (-0.5))
                dkey[:seen, :] += tn_dot(ds, q_low[band, at]) * head ** (-0.5)
                dvalue[:seen, :] += tn_dot(p.astype(B16), dout)
            dq = turned_back(jnp.concatenate(parts_q, axis=0), cos, sine)
            back, gain_part = norm_back(dq, q_pre[:, at], q_gain[...])
            low[:, at] = back.astype(B16)
            gains[1:2, :head] += gain_part
        acc[...] += nt_dot(low[...], wq[...])

    if not closing:
        heads()
        return
    pl.when(step < last)(heads)

    @pl.when(step == last)
    def _():
        dk = turned_back(dkey[...], cos, sine)
        back, gain_part = norm_back(dk, k_pre[...], k_gain[...])
        gains[2:3, :head] = gain_part
        low[:, :head] = back.astype(B16)
        low[:, head : 2 * head] = dvalue[...].astype(B16)
        acc[...] += nt_dot(low[:, :head], wk[...]) + nt_dot(low[:, head : 2 * head], wv[...])
        values = x[...].astype(F32)
        total = acc[...]
        along = jnp.sum(total * gain[...] * values, axis=1, keepdims=True)
        gains[3:4, :rows] = jnp.broadcast_to(along, (rows, 128)).T[:1]
        scale = norm_scale(values)
        row_scale[...] = scale
        gains[0:1, :] = jnp.sum(total * (values * scale), axis=0, keepdims=True)
        size = cols[0].shape[1]
        for d, piece in enumerate(cols):
            at = pl.ds(pl.multiple_of((z_ref[0] ^ d) * size, size), size)
            piece[:rows, :] = acc[:, at].astype(B16)
            piece[rows:, :] = jnp.concatenate(
                [gains[3:4, :rows].reshape(1, rows)]
                + [gains[0:1, i * size : (i + 1) * size] for i in range(parts)]
                + [gains[1:2, :size], gains[2:3, :size]]
                + [jnp.zeros((16 - 3 - parts, size), F32)],
                axis=0,
            ).astype(B16)


def attention_backward(z, seq, x, gain, wq, wk, wv, q_gain, k_gain, wo, kept, came, held):
    opening, closing = held is None, held is not None
    rows, width = x.shape
    head = wk.shape[1]
    block = 2 * head
    pairs = wq.shape[1] // block
    half = pairs // 2
    first, steps = (0, half) if opening else (half, pairs - half)
    parts = width // (wo.shape[1] // lax.axis_size("tensor"))
    q_pre, q_low, k_pre, k_low, v_low, lse, turns = kept
    whole = lambda *shape: pl.BlockSpec(shape, lambda g, z: (0,) * len(shape))
    pair_at = lambda g: first + jnp.minimum(g, steps - 1)
    column = lambda height: pl.BlockSpec((height, block), lambda g, z: (0, pair_at(g)))
    state = [whole(rows, width), whole(rows, head), whole(rows, head), whole(8, width)]
    state_shapes = [
        shaped((rows, width), F32), shaped((rows, head), F32), shaped((rows, head), F32),
        shaped((8, width), F32),
    ]
    ins = [
        seq.reshape(rows, 1), seq.reshape(1, rows), q_gain.reshape(1, head), wq, wo,
        q_pre, q_low, k_low, v_low, lse, turns,
    ]
    in_specs = [
        whole(rows, 1), whole(1, rows), whole(1, head), column(width),
        pl.BlockSpec((block, width), lambda g, z: (pair_at(g), 0)),
        column(rows), column(rows), whole(rows, head), whole(rows, head), whole(rows, 128),
        whole(rows, 2 * head),
    ]
    low_block = pl.BlockSpec((rows, block), lambda g, z: (0, g))
    if opening:
        ins = ins + list(came)
        in_specs = in_specs + [whole(rows // parts, width)] * parts
        outs = [shaped((rows, width), B16), shaped((rows, block * steps), B16)] + state_shapes
        out_specs = [whole(rows, width), low_block] + state
        scratch = [pltpu.VMEM((rows, rows), F32)]
    else:
        ins = ins + list(held) + [
            x, gain.reshape(1, width), wk, wv, k_gain.reshape(1, head), k_pre,
        ]
        in_specs = in_specs + [whole(rows, width)] + state + [
            whole(rows, width), whole(1, width), whole(width, head), whole(width, head),
            whole(1, head), whole(rows, head),
        ]
        outs = [shaped((rows + 16, width // parts), B16)] * parts + [
            shaped((rows, block * (steps + 1)), B16), shaped((rows, 1), F32),
        ]
        out_specs = [whole(rows + 16, width // parts)] * parts + [low_block, whole(rows, 1)]
        scratch = [
            pltpu.VMEM((8, width), F32),
            pltpu.VMEM((rows, rows), F32), pltpu.VMEM((rows, width), F32),
            pltpu.VMEM((rows, head), F32), pltpu.VMEM((rows, head), F32),
        ]
    return pl.pallas_call(
        functools.partial(
            backward_kernel, min(rows, 256), parts, first, opening, closing
        ),
        grid_spec=pltpu.PrefetchScalarGridSpec(
            num_scalar_prefetch=1,
            grid=(steps + closing,),
            in_specs=in_specs,
            out_specs=out_specs,
            scratch_shapes=scratch,
        ),
        out_shape=outs,
        compiler_params=params(),
        cost_estimate=cost(16),
    )(z, *ins)


def grads_in_blocks(order, left, rights):
    count = order.shape[0]
    half, high = count // 2, left.shape[1] // count
    wide = sum(v.shape[1] for v in rights)

    def kernel(order_ref, left_ref, *refs):
        right_refs, (send, keep, *whole) = refs[: len(rights)], refs[len(rights) :]
        start = 0
        for ref in right_refs if whole else ():
            end = start + ref.shape[1]
            whole[0][:, start:end] = tn_dot(left_ref[...], ref[...]).astype(B16)
            start = end
        for i in range(count):
            if whole:
                at = pl.ds(pl.multiple_of(order_ref[i] * high, high), high)
                (send, keep)[i // half][i % half] = whole[0][at, :]
                continue
            at = pl.ds(pl.multiple_of(order_ref[i] * high, high), high)
            block = left_ref[:, at]
            out, start = (send, keep)[i // half], 0
            for ref in right_refs:
                end = start + ref.shape[1]
                out[i % half, :, start:end] = tn_dot(block, ref[...]).astype(B16)
                start = end

    return pl.pallas_call(
        kernel,
        in_specs=[SMEM_SPEC] + vmem(1 + len(rights)),
        out_specs=vmem(2),
        out_shape=[shaped((half, high, wide), B16)] * 2,
        scratch_shapes=[pltpu.VMEM((left.shape[1], wide), B16)] if high % 128 else [],
        compiler_params=params(),
        cost_estimate=cost(6),
    )(order, left, *rights)


def halves_after(keep, came):
    half = keep.shape[0] // 2
    return add_low(keep[:half], came[:half]), add_low(keep[half:], came[half:])


def router_kernel(terms, experts, *refs):
    parts, (x, routes, gain, router, middle, packed, shares) = refs[:terms], refs[terms:]
    total = x[...].astype(F32)
    branch = parts[0][...].astype(F32)
    for part in parts[1:]:
        branch = branch + part[...].astype(F32)
    total = total + branch
    middle[...] = total
    width = total.shape[1]
    hidden = (total * norm_scale(total) * gain[...]).astype(B16)
    packed[:, :width] = hidden
    logits = nt_dot(hidden, router[...])
    lane = lax.broadcasted_iota(jnp.int32, logits.shape, 1)
    twin = jnp.where(lane < experts, lane, lane - experts)
    chosen = jnp.zeros(logits.shape, jnp.bool_)
    for k in range(routes.shape[1]):
        chosen = chosen | (twin == routes[:, k : k + 1])
    chosen = chosen & (lane < 2 * experts)
    peak = jnp.max(jnp.where(chosen, logits, -1e30), axis=1, keepdims=True)
    raised = jnp.where(chosen, jnp.exp(jnp.minimum(logits - peak, 0.0)), 0.0)
    share = raised / jnp.sum(jnp.where(lane < experts, raised, 0.0), axis=1, keepdims=True)
    shares[...] = share
    high = share.astype(B16).astype(F32)
    packed[:, width:] = jnp.where(lane < experts, high, share - high).astype(B16)


def row_block(height, width):
    return pl.BlockSpec((height, width), lambda g, z: (z[0], 0))


def route_rows(z, terms, x, routes, gain, router, experts):
    own, width = terms[0].shape
    extra = router.shape[0]
    whole = lambda *shape: pl.BlockSpec(shape, lambda g, z: (0,) * len(shape))
    count = len(terms)

    def kernel(z_ref, *refs):
        router_kernel(count, experts, *refs)

    return pl.pallas_call(
        kernel,
        grid_spec=pltpu.PrefetchScalarGridSpec(
            num_scalar_prefetch=1,
            grid=(1,),
            in_specs=[whole(own, width)] * count + [
                row_block(own, width), row_block(own, routes.shape[1]), whole(1, width),
                whole(extra, width),
            ],
            out_specs=[whole(own, width), whole(own, width + extra), whole(own, extra)],
        ),
        out_shape=[
            shaped((own, width), F32), shaped((own, width + extra), B16), shaped((own, extra), F32),
        ],
        compiler_params=params(),
        cost_estimate=cost(3),
    )(z, *terms, x, routes, gain.reshape(1, width), router)


def rows_back_kernel(count, experts, *refs):
    terms, (dy, middle, shares, gain, router, dbranch, sums) = refs[:count], refs[count:]
    width = middle.shape[1]
    total = terms[0][...].astype(F32)
    for term in terms[1:]:
        total = total + term[...].astype(F32)
    values = middle[...]
    share = shares[...]
    lane = lax.broadcasted_iota(jnp.int32, share.shape, 1)
    dshare = total[:, width:]
    share = jnp.where(lane < experts, share, 0.0)
    mean = jnp.sum(share * dshare, axis=1, keepdims=True)
    dlogits = (share * (dshare - mean)).astype(B16)
    scale = norm_scale(values)
    unit = values * scale
    hidden = (unit * gain[...]).astype(B16)
    dhidden = total[:, :width] + nn_dot(dlogits, router[...])
    gained = dhidden * gain[...]
    back = scale * (gained - unit * jnp.mean(gained * unit, axis=-1, keepdims=True))
    dbranch[...] = (back + dy[...].astype(F32)).astype(B16)
    grads = tn_dot(dlogits, hidden)
    sums[:experts, :] = grads[:experts, :]
    sums[experts:, :] = jnp.broadcast_to(
        jnp.sum(dhidden * unit, axis=0, keepdims=True), (8, width)
    )


def rows_back(z, terms, dy, middle, shares, gain, router, experts):
    own, width = middle.shape
    extra = router.shape[0]
    whole = lambda *shape: pl.BlockSpec(shape, lambda g, z: (0,) * len(shape))
    count = len(terms)

    def kernel(z_ref, *refs):
        rows_back_kernel(count, experts, *refs)

    return pl.pallas_call(
        kernel,
        grid_spec=pltpu.PrefetchScalarGridSpec(
            num_scalar_prefetch=1,
            grid=(1,),
            in_specs=[whole(own, width + extra)] * count + [
                row_block(own, width), whole(own, width), whole(own, extra), whole(1, width),
                whole(extra, width),
            ],
            out_specs=[whole(own, width), whole(experts + 8, width)],
        ),
        out_shape=[shaped((own, width), B16), shaped((experts + 8, width), F32)],
        compiler_params=params(),
        cost_estimate=cost(4),
    )(z, *terms, dy, middle, shares, gain.reshape(1, width), router)


def input_grad_of(z, terms, x, branch, gain, row_scale):
    rows, width = x.shape
    size = terms[0].shape[1]
    below = terms[0].shape[0] - rows
    count = len(terms)

    def kernel(z_ref, *refs):
        parts, (x_ref, branch_ref, gain_ref, scale_ref, out, small) = refs[:count], refs[count:]
        total = parts[0][...].astype(F32)
        for part in parts[1:]:
            total = total + part[...].astype(F32)
        small[...] = total[rows:, :]
        along = jnp.broadcast_to(total[rows : rows + 1, :rows], (128, rows)).T[:, :1]
        scale = scale_ref[...]
        out[...] = branch_ref[...].astype(F32) + scale * (
            total[:rows, :] * gain_ref[...]
            - x_ref[...].astype(F32) * (scale * scale * (along * (1.0 / width)))
        )

    whole = lambda *shape: pl.BlockSpec(shape, lambda g, z: (0,) * len(shape))
    column = lambda height: pl.BlockSpec((height, size), lambda g, z: (0, z[0]))
    return pl.pallas_call(
        kernel,
        grid_spec=pltpu.PrefetchScalarGridSpec(
            num_scalar_prefetch=1,
            grid=(1,),
            in_specs=[whole(rows + below, size)] * count + [
                column(rows), column(rows), column(1), whole(rows, 1),
            ],
            out_specs=[whole(rows, size), whole(below, size)],
        ),
        out_shape=[shaped((rows, size), F32), shaped((below, size), F32)],
        compiler_params=params(),
        cost_estimate=cost(3),
    )(z, *terms, x, branch, gain.reshape(1, width), row_scale)


def expert_kernel(places, group, slots, hidden, experts, *refs):
    parts = len(places)
    z_ref, ids_ref, refs = refs[0], refs[1], refs[2:]
    packed, refs = refs[:parts], refs[parts:]
    dy, refs = refs[0], refs[1:]
    weights, refs = refs[: 3 * group], refs[3 * group :]
    backs, refs = refs[:parts], refs[parts:]
    held, dgu_out, act_out, gate_up, down, dgu_buf, act_buf, total, sems, out_sems = refs
    rows, width = dy.shape
    pair = 2 * hidden
    size = rows // parts
    extra = held.shape[1] - width

    def fetch(d):
        slot = d % slots
        gate, up, dn = weights[3 * d : 3 * d + 3]
        return [
            pltpu.make_async_copy(gate, gate_up.at[slot, :pair], sems.at[0, slot]),
            pltpu.make_async_copy(up, gate_up.at[slot, pair:], sems.at[1, slot]),
            pltpu.make_async_copy(dn, down.at[slot], sems.at[2, slot]),
        ]

    def store(d):
        return [
            pltpu.make_async_copy(dgu_buf.at[d % 2], dgu_out.at[d], out_sems.at[0, d % 2]),
            pltpu.make_async_copy(act_buf.at[d % 2], act_out.at[d], out_sems.at[1, d % 2]),
        ]

    for copy in fetch(0):
        copy.start()
    for d in range(1, min(slots, group)):
        for copy in fetch(d):
            copy.start()

    def rows_of(d):
        return pl.ds(pl.multiple_of((z_ref[0] ^ d) * size, size), size)

    for i, d in enumerate(places):
        held[rows_of(d), :] = packed[i][...]
    shares = held[:, width:].astype(F32)
    lane = lax.broadcasted_iota(jnp.int32, (rows, extra), 1)
    first = lax.broadcasted_iota(jnp.int32, (rows, pair), 1) < hidden

    def share_of(expert):
        mine = (lane == expert) | (lane == expert + experts)
        return jnp.sum(jnp.where(mine, shares, 0.0), axis=1, keepdims=True)

    dshares = jnp.zeros((rows, extra), F32)
    for d in range(group):
        slot = d % slots
        for copy in fetch(d):
            copy.wait()
        id_a, id_b = ids_ref[2 * d], ids_ref[2 * d + 1]
        both = nt_dot(held[:, :width], gate_up[slot])
        raw = nt_dot(dy[...], down[slot])
        gate, up = both[:, :pair], both[:, pair:]
        share = jnp.where(first, share_of(id_a), share_of(id_b))
        sig = 1.0 / (1.0 + jnp.exp(-gate))
        silu = gate * sig
        act = (silu * up).astype(B16).astype(F32)
        product = act * raw
        part_a = jnp.sum(jnp.where(first, product, 0.0), axis=1, keepdims=True)
        part_b = jnp.sum(jnp.where(first, 0.0, product), axis=1, keepdims=True)
        dshares = dshares + jnp.where(lane == id_a, part_a, 0.0)
        dshares = dshares + jnp.where(lane == id_b, part_b, 0.0)
        dact = share * raw
        dgate = dact * up * (sig * (1.0 + gate * (1.0 - sig)))
        dup = dact * silu
        if d >= 2:
            for copy in store(d - 2):
                copy.wait()
        dgu_buf[d % 2, :, :pair] = dgate.astype(B16)
        dgu_buf[d % 2, :, pair:] = dup.astype(B16)
        act_buf[d % 2] = (share * act).astype(B16)
        for copy in store(d):
            copy.start()
        term = nn_dot(dgu_buf[d % 2], gate_up[slot])
        total[...] = term if d == 0 else total[...] + term
        if d + slots < group:
            for copy in fetch(d + slots):
                copy.start()
    for i, d in enumerate(places):
        backs[i][:, :width] = total[rows_of(d), :].astype(B16)
    total[:, :extra] = dshares
    for i, d in enumerate(places):
        backs[i][:, width:] = total[rows_of(d), :extra].astype(B16)
    for d in range(max(0, group - 2), group):
        for copy in store(d):
            copy.wait()


def expert_pass(z, ids, places, packed, dy, weights, experts):
    width = dy.shape[1]
    parts = len(places)
    size, full = packed[0].shape
    rows = size * parts
    group = len(weights)
    pair = weights[0][0].shape[0]
    slots = min(group, 4)
    out = pl.pallas_call(
        functools.partial(expert_kernel, tuple(places), group, slots, pair // 2, experts),
        in_specs=[SMEM_SPEC, SMEM_SPEC] + vmem(parts + 1) + hbm(3 * group),
        out_specs=vmem(parts + 1) + hbm(2),
        out_shape=[shaped((size, full), B16)] * parts + [
            shaped((rows, full), B16),
            shaped((group, rows, 2 * pair), B16),
            shaped((group, rows, pair), B16),
        ],
        scratch_shapes=[
            pltpu.VMEM((slots, 2 * pair, width), B16),
            pltpu.VMEM((slots, pair, width), B16),
            pltpu.VMEM((2, rows, 2 * pair), B16),
            pltpu.VMEM((2, rows, pair), B16),
            pltpu.VMEM((rows, width), F32),
            pltpu.SemaphoreType.DMA((3, slots)),
            pltpu.SemaphoreType.DMA((2, 2)),
        ],
        compiler_params=params(58),
        cost_estimate=cost(31),
    )(z, ids, *packed, dy, *[w for three in weights for w in three])
    return dict(zip(places, out[:parts])), out[parts:]


def outputs_kernel(parts, sources, group, z_ref, middle, *refs):
    acts, refs = refs[:sources], refs[sources:]
    downs, outs, total = refs[:group], refs[group:-1], refs[-1]
    size = outs[0].shape[1]
    for s in range(sources):
        value = nn_dot(acts[s][0], downs[0][...])
        for d in range(1, group):
            value = value + nn_dot(acts[s][d], downs[d][...])
        total[...] = value
        if s == 0:
            own = middle.shape[0]
            total[pl.ds(pl.multiple_of(z_ref[0] * own, own), own), :] += middle[...]
        for d in range(parts):
            at = pl.ds(pl.multiple_of((z_ref[0] ^ d) * size, size), size)
            outs[s * parts + d][...] = total[:, at].astype(B16)


def expert_outputs(z, middle, acts, downs, parts):
    group, rows, pair = acts[0].shape
    width = downs[0].shape[1]
    count = len(acts) * parts
    return pl.pallas_call(
        functools.partial(outputs_kernel, parts, len(acts), group),
        in_specs=[SMEM_SPEC] + vmem(1 + len(acts) + group),
        out_specs=vmem(count),
        out_shape=[shaped((rows, width // parts), B16)] * count,
        scratch_shapes=[pltpu.VMEM((rows, width), F32)],
        compiler_params=params(),
        cost_estimate=cost(10),
    )(z, middle, *acts, *downs)


def grads_kernel(sources, *refs):
    ins, out = refs[:-1], refs[-1]
    width = out.shape[1]

    def write(part):
        total = 0.0
        for s in range(sources):
            held, dy, dgu, act = ins[4 * s : 4 * s + 4]
            if part < 2:
                total = total + tn_dot(dgu[0], held[:, :width])
            else:
                total = total + tn_dot(act[0], dy[...])
        out[...] = total.astype(B16)

    step = pl.program_id(0)
    pl.when(step < 2)(functools.partial(write, 0))
    pl.when(step == 2)(functools.partial(write, 2))


def expert_grads(distance, sources):
    pair, width = sources[0][3].shape[2], sources[0][1].shape[1]
    whole = lambda *shape: pl.BlockSpec(shape, lambda g: (0,) * len(shape))
    return pl.pallas_call(
        functools.partial(grads_kernel, len(sources)),
        grid=(3,),
        in_specs=[
            spec
            for held, dy, dgu, act in sources
            for spec in (
                whole(*held.shape),
                whole(*dy.shape),
                pl.BlockSpec((1, held.shape[0], pair), lambda g: (distance, 0, jnp.minimum(g, 1))),
                pl.BlockSpec((1, held.shape[0], pair), lambda g: (distance, 0, 0)),
            )
        ],
        out_specs=pl.BlockSpec((pair, width), lambda g: (g, 0)),
        out_shape=shaped((3 * pair, width), B16),
        compiler_params=params(),
        cost_estimate=cost(11),
    )(*[v for source in sources for v in source])


def sum_of_grads(wholes, pieces):
    rows, width = wholes[0].shape
    block = min(width, 512)
    size = pieces[0].shape[0]
    count = len(wholes)
    each = rows // 3

    def kernel(*refs):
        parts, refs = refs[:count], refs[count:]
        more, outs = refs[:-3], refs[-3:]
        for i, piece in enumerate(more):
            total = piece[...].astype(F32)
            for part in parts:
                total = total + part[i * size : (i + 1) * size, :].astype(F32)
            at = i * size % each
            outs[i * size // each][at : at + size, :] = total

    line = lambda height: pl.BlockSpec((height, block), lambda g: (0, g))
    return pl.pallas_call(
        kernel,
        grid=(width // block,),
        in_specs=[line(rows)] * count + [line(size)] * len(pieces),
        out_specs=[line(each)] * 3,
        out_shape=[shaped((each, width), F32)] * 3,
        compiler_params=params(),
        cost_estimate=cost(8),
    )(*wholes, *pieces)


def per_device(
    tokens,
    sequence_numbers,
    routes,
    attn_gain,
    w_query,
    key_projection,
    value_projection,
    query_gain,
    key_gain,
    w_out,
    moe_gain,
    w_router,
    w_gate,
    w_up,
    w_down,
    cotangent,
):
    tok_count, model_width = tokens.shape
    head_dim = query_gain.shape[0]
    tensor_size = lax.axis_size("tensor")
    tensor_pos = lax.axis_index("tensor")
    expert_size = lax.axis_size("expert")
    expert_pos = lax.axis_index("expert")
    local_experts, _, hidden = w_gate.shape
    experts = local_experts * expert_size
    pair = local_experts * hidden
    group = 2 << ((expert_size // 2).bit_length() // 2)
    rounds = expert_size // group
    own_rows = tok_count // tensor_size
    everyone = list(range(tensor_size))
    z = tensor_pos.astype(jnp.int32).reshape(1)

    weights = [
        {0: jnp.swapaxes(w_gate, 1, 2).reshape(pair, model_width)},
        {0: jnp.swapaxes(w_up, 1, 2).reshape(pair, model_width)},
        {0: w_down.reshape(pair, model_width)},
    ]
    for held in weights:
        for bit in reversed(range(1, group.bit_length() - 1)):
            held.update({d ^ (1 << bit): swap(v, "expert", 1 << bit) for d, v in list(held.items())})
    ids = jnp.concatenate(
        [(expert_pos ^ d) * local_experts + jnp.arange(local_experts) for d in range(group)]
    ).astype(jnp.int32)
    dy_own = lax.all_gather(cotangent, "tensor", axis=1, tiled=True)

    attention = (
        z, sequence_numbers, tokens, attn_gain, w_query, key_projection, value_projection,
        query_gain, key_gain, w_out,
    )
    branch_parts, kept = attention_forward(*attention, tensor_size)
    first_hidden, attended_low = kept[0], kept[6]
    kept = kept[1:6] + kept[7:]
    branch_came = exchange_near(branch_parts, "tensor")
    for d in everyone[2::2]:
        branch_came[d], weights[0] = together(branch_came[d], weights[0])
    dy_own = after(dy_own, branch_came[2])
    dy_of = [dy_own] + [swap(dy_own, "expert", group * r) for r in range(1, rounds)]
    terms = [branch_parts[0], branch_came[0]] + further_terms(branch_parts, branch_came, "tensor")
    terms, weights[1] = together(terms, weights[1])

    router_rows = jnp.swapaxes(w_router, 0, 1)
    spare = -(2 * experts) % 128
    router_rows = jnp.concatenate(
        [router_rows, router_rows, jnp.zeros((spare, model_width), B16)], axis=0
    )
    middle, packed_rows, shares = route_rows(
        z, terms, tokens, routes, moe_gain, router_rows, experts
    )
    for i in range(2):
        weights[i] = after(weights[i], packed_rows)
        weights[i].update({d ^ 1: swap(v, "expert", 1) for d, v in list(weights[i].items())})
    packed_of = [{0: packed_rows}] + [
        {0: swap(packed_rows, "expert", group * r)} for r in range(1, rounds)
    ]
    top = bits_of("tensor") - 1
    first = {1 << bit: swap(packed_rows, "tensor", 1 << bit) for bit in range(top + 1)}
    first, weights[2] = together(first, weights[2])
    weights[2].update({d ^ 1: swap(v, "expert", 1) for d, v in list(weights[2].items())})
    packed_of[0].update(first)
    for bit in reversed(range(top)):
        came = {
            d | 1 << bit: swap(v, "tensor", 1 << bit)
            for d, v in packed_of[0].items() if d and not d & ((2 << bit) - 1)
        }
        packed_of[0].update(after(came, [p[0] for p in packed_of[1:]], dy_of[1:]))
    for r in range(1, rounds):
        packed_of[r].update(
            {d: swap(v, "expert", group * r) for d, v in packed_of[0].items() if d}
        )
    weights = [[held[d] for held in weights] for d in range(group)]

    far = [d for d in everyone if d & 1][::-1]
    near = [d for d in everyone if not d & 1][::-1]
    back, sources = [], []
    for r in range(rounds):
        part, extra = expert_pass(
            after(z, [b[0] for b in back]), ids, everyone,
            [packed_of[r][d] for d in everyone], dy_of[r], weights, experts,
        )
        if r:
            part = {d: swap(part[d], "expert", group * r) for d in far + near}
        back.append(part)
        sources.append((extra[0], dy_of[r], extra[1], extra[2]))

    downs = [w[2] for w in weights]
    joined = [None] * tensor_size
    made, odd, high, passed = {}, {}, {}, {}
    mask = group // 2
    outs = expert_outputs(
        z, middle, [source[3] for source in sources], downs, tensor_size
    )
    for place in far:
        joined[place] = add_low(*after([b[place] for b in back], outs[0]))
    last = [joined[place] for place in far]
    for d in range(group - 1, mask - 1, -1):
        made[d] = expert_grads(d, after(sources, last))
        last = [made[d]]
        if d == group - 1:
            for place in near[:-1]:
                joined[place] = add_low(*after([b[place] for b in back], last))
                last = last + [joined[place]]
    for d in range(group - 1, mask - 1, -2):
        odd[d - 1] = swap(after(made[d], last), "expert", 1)
    for d in range(group - 2, mask - 1, -2):
        mine_all, theirs_all = after([made[d], odd[d]], last)
        high[d] = [
            add_low(mine_all[i * hidden : (i + 1) * hidden], theirs_all[i * hidden : (i + 1) * hidden])
            for i in range(3 * local_experts)
        ]
        passed[d - mask] = [swap(v, "expert", mask) for v in high[d]]
    out_own = outs[:tensor_size]
    out_came = [
        {d: swap(outs[r * tensor_size + d], "expert", group * r) for d in far + near}
        for r in range(1, rounds)
    ]

    def pieces_at(*places):
        return [v[i] for v in passed.values() for i in places]

    back_terms = [b[0] for b in back] + scatter_terms_of(joined, "tensor")
    shape = (local_experts, hidden, model_width)

    back_terms = after(
        back_terms, last, [came[far[0]] for came in out_came]
    )
    dbranch, row_sums = rows_back(
        z, back_terms, dy_own, middle, shares, moe_gain, router_rows, experts
    )
    row_sums = row_sums[: experts + 1]
    lower = list(range(group // 2 - 1, -1, -1))
    pieces, last = {0: dbranch}, dbranch
    for bit in reversed(range(bits_of("tensor"))):
        came = {d ^ (1 << bit): swap(v, "tensor", 1 << bit) for d, v in pieces.items()}
        share_lower = -(-len(lower) // bits_of("tensor"))
        place = bits_of("tensor") - 1 - bit
        for d in lower[place * share_lower : (place + 1) * share_lower]:
            made[d] = expert_grads(d, after(sources, last))
            if d & 1:
                odd[d - 1] = swap(made[d], "expert", 1)
            last = made[d]
        came = after(came, last)
        if bit:
            came = after(came, [came_r[far[-1]] for came_r in out_came], pieces_at(0))
        else:
            came = after(came, pieces_at(1), [came_r[d] for came_r in out_came for d in near if d])
        pieces.update(came)
        last = came
    dbranch_pieces = [pieces[d] for d in everyone]
    mine = {d: [made[d], odd[d]] for d in range(0, mask, 2)}
    theirs = passed
    while mask > 2:
        sums = {d: add_low(*v, jnp.concatenate(theirs[d], axis=0)) for d, v in mine.items()}
        mask //= 2
        theirs = {
            d - mask: [
                swap(sums[d][i * hidden : (i + 1) * hidden], "expert", mask)
                for i in range(3 * local_experts)
            ]
            for d in sums if d >= mask
        }
        mine = {d: [sums[d]] for d in sums if d < mask}
    out_parts = [None] * tensor_size
    for d in far:
        came = after([came_r[d] for came_r in out_came], dbranch_pieces)
        out_parts[d] = add_low(out_own[d], *came)
    out_far = exchange_near(out_parts, "tensor")

    branch_low = jnp.zeros((tok_count, model_width), B16)
    for d, v in enumerate(dbranch_pieces):
        at = (tensor_pos ^ d) * v.shape[0]
        branch_low = lax.dynamic_update_slice_in_dim(branch_low, v, at, 0)
    order = expert_pos ^ jnp.asarray(
        list(range(1, expert_size, 2)) + list(range(0, expert_size, 2)), jnp.int32
    )
    far_bits = list(reversed(range(1, bits_of("expert"))))
    wo_send, wo_keep = grads_in_blocks(order, branch_low, [attended_low])
    wo_came = swap(wo_send, "expert", 1)
    dbranch_pieces = after(dbranch_pieces, wo_keep)
    branch_low, low_first, *held = attention_backward(*attention, kept, dbranch_pieces, None)
    wo_keep, wo_send = halves_after(wo_keep, wo_came)
    held, out_came, out_far, theirs[0][2], wo_send, wo_keep = together(
        held, out_came, out_far, theirs[0][2], wo_send, wo_keep
    )
    wo_came = swap(wo_send, "expert", 1 << far_bits[0])
    for d in near:
        if d:
            out_parts[d] = add_low(out_own[d], *[came_r[d] for came_r in out_came])
    out_terms = [out_own[0]] + [came_r[0] for came_r in out_came]
    out_came = out_far
    out_sums = {d: add_low(out_parts[d], v) if d else None for d, v in out_came.items()}
    held = after(held, out_sums)
    out_terms = out_terms + [out_came[0]] + passed_on(out_sums, "tensor")
    *cols_out, low_last, row_scale = attention_backward(
        *attention, kept, None, [branch_low] + held
    )
    col_parts = cols_out
    low_last, theirs[0][3], wo_came, out_terms = together(
        low_last, theirs[0][3], wo_came, out_terms
    )
    for bit in far_bits[1:]:
        wo_keep, wo_send = halves_after(wo_keep, wo_came)
        wo_came = swap(wo_send, "expert", 1 << bit)
    col_came = exchange_near(col_parts, "tensor")
    q_send, q_keep = grads_in_blocks(order, first_hidden, [low_first, low_last])
    q_came = swap(q_send, "expert", 1)
    q_keep, q_send = halves_after(q_keep, q_came)
    q_came = swap(q_send, "expert", 1 << far_bits[0])
    col_came = after(col_came, theirs[0][4], q_send, wo_came)
    gate_flat, up_flat, down_flat = sum_of_grads(mine[0], theirs[0])
    gate_grad = jnp.swapaxes(gate_flat.reshape(shape), 1, 2)
    up_grad = jnp.swapaxes(up_flat.reshape(shape), 1, 2)
    down_grad = down_flat.reshape(shape)
    col_sums = {d: add_low(col_parts[d], v) if d else None for d, v in col_came.items()}
    q_came = after(q_came, col_sums)
    col_terms = [col_parts[0], col_came[0]] + passed_on(col_sums, "tensor")
    for bit in far_bits[1:]:
        q_keep, q_send = halves_after(q_keep, q_came)
        q_came = swap(q_send, "expert", 1 << bit)
    out_weight_grad = (wo_keep[0].astype(F32) + wo_came[0].astype(F32)).T
    col_terms = after(col_terms, q_came, gate_flat)
    input_grad, small = input_grad_of(z, col_terms, tokens, branch_low, attn_gain, row_scale)
    gains = small[1 : 1 + tensor_size].reshape(1, model_width)
    qkv = q_keep[0].astype(F32) + q_came[0].astype(F32)
    q_size = w_query.shape[1]

    def share_of_sum(small):
        small = small.reshape((small.shape[0],) + (2,) * bits_of("expert") + (-1,))
        for bit in range(bits_of("expert")):
            dim = small.ndim - 2
            mine = (expert_pos >> bit) & 1
            send = lax.dynamic_index_in_dim(small, 1 - mine, dim, False)
            keep = lax.dynamic_index_in_dim(small, mine, dim, False)
            small = keep + swap(send, "expert", 1 << bit)
        return small

    columns_each = model_width // expert_size
    head_each = head_dim // expert_size
    spread = jnp.pad(
        small[1 + tensor_size : 3 + tensor_size, :head_dim].reshape(2, expert_size, head_each),
        ((0, 0), (0, 0), (0, columns_each - head_each)),
    )
    small = share_of_sum(
        jnp.concatenate([gains, spread.reshape(2, model_width), row_sums], axis=0)
    )
    row_share = sum_everywhere(small[3:], "tensor")
    mixed = functools.reduce(jnp.add, [t.astype(F32) for t in out_terms])
    block_out = mixed.astype(B16)

    return (
        block_out,
        input_grad,
        small[0],
        qkv[:, :q_size],
        qkv[:, q_size : q_size + head_dim],
        qkv[:, q_size + head_dim :],
        small[1, :head_each],
        small[2, :head_each],
        out_weight_grad,
        row_share[experts],
        jnp.swapaxes(row_share[:experts], 0, 1),
        gate_grad,
        up_grad,
        down_grad,
    )


def solution(mesh):
    placed = (
        P("expert", None),
        P("expert"),
        P("expert", None),
        P(),
        P(None, "tensor"),
        P(None, "tensor"),
        P(None, "tensor"),
        P(),
        P(),
        P("tensor", None),
        P(),
        P(),
        P("expert", None, "tensor"),
        P("expert", None, "tensor"),
        P("expert", "tensor", None),
        P("expert", "tensor"),
    )
    return jax.shard_map(
        per_device,
        mesh=mesh,
        in_specs=placed,
        out_specs=(
            P("expert", "tensor"),
            P("expert", "tensor"),
            P("expert"),
            P("expert", "tensor"),
            P("expert", "tensor"),
            P("expert", "tensor"),
            P("expert"),
            P("expert"),
            P("tensor", "expert"),
            P("expert"),
            P("expert", None),
            P("expert", None, "tensor"),
            P("expert", None, "tensor"),
            P("expert", "tensor", None),
        ),
        check_vma=False,
    )
```
